32 devices in a mesh: row: 4 (over y, core), col: 8 (over z, x).
Axes of the slice: x: 2, y: 2, z: 4, core: 2. Of those that a mesh axis runs over, the one named last changes fastest.
Arguments:
- images: bfloat16 [1024, 1024], P(('row', 'col')), may hold values from -6 to 6
- texts: bfloat16 [1024, 1024], P(('row', 'col')), may hold values from -6 to 6
- loss_weights: float32 [2], replicated, may hold values from 0.5 to 1.5
Outputs:
- grad_images: float32 [1024, 1024], P(('row', 'col'))
- grad_texts: float32 [1024, 1024], P(('row', 'col'))
The draws below stay inside these ranges and needn't reach their ends.
All inputs are finite; a program needn't handle non-finite values.
Results may differ from the reference program's by a relative error of at most 0.0013.
Values may be sent and summed in bfloat16 or wider, within the bound.
No kernel may reach another device: no remote copies, remote signals or barrier semaphores. Data moves between devices by JAX's collectives and lax.ppermute only.
A program may use at most 64 MiB of HBM per device.

```python
import math
import jax
import jax.numpy as jnp
from jax import lax

D = 1024
BATCH = 1024
ROW_BLOCK = 256


def levels(rng, extent, shards, least, high):
    loudness, own = 1.0, jax.random.fold_in(rng, 6)
    for dim, parts in shards:
        draws = jnp.exp(jax.random.uniform(jax.random.fold_in(own, dim), (parts,), jnp.float32, least / len(shards), high / len(shards)))
        loudness = loudness * jnp.repeat(draws, extent[dim] // parts).reshape([-1 if axis == dim else 1 for axis in range(len(extent))])
    return loudness


def bell_draw(stream_key, extent, scale, limit, pieces=(), kind=jnp.bfloat16):
    result = scale * jax.random.normal(stream_key, extent, jnp.float32)
    if pieces:
        result = result * levels(stream_key, extent, pieces, -0.22, 0.18)
    return jnp.clip(result, -limit, limit).astype(kind)


def setup_inputs(seed: int = 0) -> dict:
    streams_of = jax.random.split(jax.random.key(seed), 4)
    images = bell_draw(streams_of[0], (BATCH, D), 1.0, 6.0, ((0, 32),))
    texts = bell_draw(streams_of[1], (BATCH, D), 1.0, 6.0, ((0, 32),))
    loss_weights = jnp.clip(jax.random.uniform(streams_of[2], (2,), jnp.float32, 0.5, 1.5), 0.5, 1.5)
    return {"images": images, "texts": texts, "loss_weights": loss_weights}


def reference(images, texts, loss_weights):
    scale = 1.0 / math.sqrt(D * BATCH)
    cross_scale = loss_weights[0] * scale
    inner_scale = loss_weights[1] * scale
    stacked = jnp.concatenate([images, texts], axis=1).reshape(BATCH // ROW_BLOCK, ROW_BLOCK, 2 * D)

    def one_block(rows):
        rows_img = rows[:, :D]
        rows_txt = rows[:, D:]
        cross = jnp.dot(rows_img, texts.T, preferred_element_type=jnp.float32) - jnp.dot(rows_txt, images.T, preferred_element_type=jnp.float32)
        inmodal = jnp.dot(rows_img, images.T, preferred_element_type=jnp.float32) - jnp.dot(rows_txt, texts.T, preferred_element_type=jnp.float32)
        p_mat = (cross * cross_scale).astype(jnp.bfloat16)
        q_mat = (inmodal * inner_scale).astype(jnp.bfloat16)
        grad_img = jnp.dot(p_mat, texts, preferred_element_type=jnp.float32) + jnp.dot(q_mat, images, preferred_element_type=jnp.float32)
        grad_txt = -jnp.dot(p_mat, images, preferred_element_type=jnp.float32) - jnp.dot(q_mat, texts, preferred_element_type=jnp.float32)
        return (grad_img, grad_txt)
    grad_img, grad_txt = lax.map(one_block, stacked)
    return (grad_img.reshape(BATCH, D), grad_txt.reshape(BATCH, D))
```

```python
import functools
import math

import jax
import jax.numpy as jnp
from jax import lax
from jax.experimental import pallas as pl
from jax.experimental.pallas import tpu as pltpu
from jax.sharding import PartitionSpec as P


def halves(count):
    inner = 2 if count % 2 == 0 else 1
    return count // inner, inner


def outer_shift(count, step):
    outer, inner = halves(count)
    return [(i, (i // inner + step) % outer * inner + i % inner) for i in range(count)]


def inner_shift(count, step):
    _, inner = halves(count)
    return [(i, i // inner * inner + (i + step) % inner) for i in range(count)]


def both_shift(count, j, k):
    outer, inner = halves(count)
    return [((i // inner + j) % outer * inner + (i + k) % inner, i) for i in range(count)]


def stacked(refs, part):
    return jnp.concatenate([ref[part] for ref in refs], axis=0)


def dot(a, b, dims):
    return lax.dot_general(a, b, (dims, ((), ())), preferred_element_type=jnp.float32)


def block_kernel(scale, n_own, n_keys, weights, *refs):
    own, keys, outs = refs[:n_own], refs[n_own : n_own + n_keys], refs[n_own + n_keys :]
    nt = ((1,), (1,))
    nn = ((1,), (0,))
    img, txt = stacked(own, 0), stacked(own, 1)
    key_img, key_txt = stacked(keys, 0), stacked(keys, 1)
    cross = dot(img, key_txt, nt) - dot(txt, key_img, nt)
    inmodal = dot(img, key_img, nt) - dot(txt, key_txt, nt)
    p_mat = (cross * (weights[0] * scale)).astype(jnp.bfloat16)
    q_mat = (inmodal * (weights[1] * scale)).astype(jnp.bfloat16)
    grad_img = dot(p_mat, key_txt, nn) + dot(q_mat, key_img, nn)
    grad_txt = -dot(p_mat, key_img, nn) - dot(q_mat, key_txt, nn)
    rows = own[0].shape[1]
    for i, out in enumerate(outs):
        out[0] = grad_img[i * rows : (i + 1) * rows]
        out[1] = grad_txt[i * rows : (i + 1) * rows]


def partials(own, keys, weights, scale):
    vmem = pl.BlockSpec(memory_space=pltpu.VMEM)
    smem = pl.BlockSpec(memory_space=pltpu.SMEM)
    return pl.pallas_call(
        functools.partial(block_kernel, scale, len(own), len(keys)),
        out_shape=[jax.ShapeDtypeStruct(x.shape, jnp.float32) for x in own],
        in_specs=[smem] + [vmem] * (len(own) + len(keys)),
        out_specs=[vmem] * len(own),
        compiler_params=pltpu.CompilerParams(vmem_limit_bytes=48 * 2**20),
    )(weights, *own, *keys)


def local(images, texts, loss_weights):
    n_row, n_col = lax.axis_size("row"), lax.axis_size("col")
    row_outer, row_inner = halves(n_row)
    col_outer, col_inner = halves(n_col)
    width = images.shape[1]
    batch = images.shape[0] * n_row * n_col
    scale = 1.0 / math.sqrt(width * batch)
    own = jnp.stack([images, texts])

    line = [own] + [lax.ppermute(own, "col", outer_shift(n_col, k)) for k in range(1, col_outer)]
    keys = list(line)
    for k in range(1, col_inner):
        keys += [lax.ppermute(block, "col", inner_shift(n_col, k)) for block in line]

    column = []
    for j in range(row_outer):
        for k in range(row_inner):
            src = both_shift(n_row, j, k)
            column.append(lax.ppermute(own, "row", src) if j or k else own)

    parts = partials(column, keys, loss_weights, scale)
    sums = []
    for j in reversed(range(row_outer)):
        total = parts[j * row_inner]
        for k in range(1, row_inner):
            total = total + lax.ppermute(parts[j * row_inner + k], "row", inner_shift(n_row, k))
        sums.insert(0, total)
    total = sums[0]
    for j in range(1, row_outer):
        total = total + lax.ppermute(sums[j], "row", outer_shift(n_row, j))
    return total[0], total[1]


def solution(mesh):
    in_specs = (P(("row", "col"), None), P(("row", "col"), None), P())
    out_specs = (P(("row", "col"), None), P(("row", "col"), None))
    return jax.shard_map(local, mesh=mesh, in_specs=in_specs, out_specs=out_specs, check_vma=False)
```

```python
import functools
import math

import jax
import jax.numpy as jnp
from jax import lax
from jax.experimental import pallas as pl
from jax.experimental.pallas import tpu as pltpu
from jax.sharding import PartitionSpec as P


def halves(count):
    inner = 2 if count % 2 == 0 else 1
    return count // inner, inner


def outer_shift(count, step):
    outer, inner = halves(count)
    return [(i, (i // inner + step) % outer * inner + i % inner) for i in range(count)]


def outer_ring(count):
    outer, inner = halves(count)
    odd, even = list(range(1, outer, 2)), list(range(0, outer, 2))
    ring = odd + even[::-1]
    after = {a: ring[(i + 1) % outer] for i, a in enumerate(ring)}
    return [(i, after[i // inner] * inner + i % inner) for i in range(count)]


def inner_shift(count, step):
    _, inner = halves(count)
    return [(i, i // inner * inner + (i + step) % inner) for i in range(count)]


def both_shift(count, j, k):
    outer, inner = halves(count)
    return [((i // inner + j) % outer * inner + (i + k) % inner, i) for i in range(count)]


def stacked(refs, part):
    return jnp.concatenate([ref[part] for ref in refs], axis=0)


def dot(a, b, dims):
    return lax.dot_general(a, b, (dims, ((), ())), preferred_element_type=jnp.float32)


def block_kernel(scale, n_own, n_keys, weights, *refs):
    own, keys, outs = refs[:n_own], refs[n_own : n_own + n_keys], refs[n_own + n_keys :]
    nt = ((1,), (1,))
    nn = ((1,), (0,))
    img, txt = stacked(own, 0), stacked(own, 1)
    key_img, key_txt = stacked(keys, 0), stacked(keys, 1)
    cross = dot(img, key_txt, nt) - dot(txt, key_img, nt)
    inmodal = dot(img, key_img, nt) - dot(txt, key_txt, nt)
    p_mat = (cross * (weights[0] * scale)).astype(jnp.bfloat16)
    q_mat = (inmodal * (weights[1] * scale)).astype(jnp.bfloat16)
    grad_img = dot(p_mat, key_txt, nn) + dot(q_mat, key_img, nn)
    grad_txt = -dot(p_mat, key_img, nn) - dot(q_mat, key_txt, nn)
    rows = own[0].shape[1]
    for i, out in enumerate(outs):
        out[0] = grad_img[i * rows : (i + 1) * rows]
        out[1] = grad_txt[i * rows : (i + 1) * rows]


def partials(own, keys, weights, scale):
    vmem = pl.BlockSpec(memory_space=pltpu.VMEM)
    smem = pl.BlockSpec(memory_space=pltpu.SMEM)
    return pl.pallas_call(
        functools.partial(block_kernel, scale, len(own), len(keys)),
        out_shape=[jax.ShapeDtypeStruct(x.shape, jnp.float32) for x in own],
        in_specs=[smem] + [vmem] * (len(own) + len(keys)),
        out_specs=[vmem] * len(own),
        compiler_params=pltpu.CompilerParams(vmem_limit_bytes=48 * 2**20),
    )(weights, *own, *keys)


def local(images, texts, loss_weights):
    n_row, n_col = lax.axis_size("row"), lax.axis_size("col")
    row_outer, row_inner = halves(n_row)
    col_outer, col_inner = halves(n_col)
    width = images.shape[1]
    batch = images.shape[0] * n_row * n_col
    scale = 1.0 / math.sqrt(width * batch)
    own = jnp.stack([images, texts])

    others = [(j, k) for j in range(row_outer) for k in range(row_inner) if j or k]
    per_round = -(-len(others) // max(col_outer - 1, 1))
    keys, column, block, mine = [own], {(0, 0): own}, own, own
    for step in range(col_outer):
        arrived, passed = block, []
        if step + 1 < col_outer:
            arrived = lax.ppermute(block, "col", outer_ring(n_col))
        for k in range(1, col_inner):
            passed.append(lax.ppermute(block, "col", inner_shift(n_col, k)))
        for j, k in others[step * per_round : (step + 1) * per_round]:
            column[j, k] = lax.ppermute(mine, "row", both_shift(n_row, j, k))
        if step + 1 < col_outer:
            block, passed, mine = lax.optimization_barrier((arrived, passed, mine))
            keys.append(block)
        keys += passed
    column = [column[j, k] for j in range(row_outer) for k in range(row_inner)]

    parts = partials(column, keys, loss_weights, scale)
    sums = []
    for j in reversed(range(row_outer)):
        total = parts[j * row_inner]
        for k in range(1, row_inner):
            total = total + lax.ppermute(parts[j * row_inner + k], "row", inner_shift(n_row, k))
        sums.insert(0, total)
    total = sums[0]
    for j in range(1, row_outer):
        total = total + lax.ppermute(sums[j], "row", outer_shift(n_row, j))
    return total[0], total[1]


def solution(mesh):
    in_specs = (P(("row", "col"), None), P(("row", "col"), None), P())
    out_specs = (P(("row", "col"), None), P(("row", "col"), None))
    return jax.shard_map(local, mesh=mesh, in_specs=in_specs, out_specs=out_specs, check_vma=False)
```

```python
import functools
import math

import jax
import jax.numpy as jnp
from jax import lax
from jax.experimental import pallas as pl
from jax.experimental.pallas import tpu as pltpu
from jax.sharding import PartitionSpec as P


def halves(count):
    inner = 2 if count % 2 == 0 else 1
    return count // inner, inner


def outer_shift(count, step):
    outer, inner = halves(count)
    return [(i, (i // inner + step) % outer * inner + i % inner) for i in range(count)]


def outer_ring(count):
    outer, inner = halves(count)
    odd, even = list(range(1, outer, 2)), list(range(0, outer, 2))
    ring = odd + even[::-1]
    after = {a: ring[(i + 1) % outer] for i, a in enumerate(ring)}
    return [(i, after[i // inner] * inner + i % inner) for i in range(count)]


def inner_shift(count, step):
    _, inner = halves(count)
    return [(i, i // inner * inner + (i + step) % inner) for i in range(count)]


def both_shift(count, j, k):
    outer, inner = halves(count)
    return [((i // inner + j) % outer * inner + (i + k) % inner, i) for i in range(count)]


def stacked(refs):
    return jnp.concatenate([ref[...] for ref in refs], axis=0)


def dot(a, b, dims):
    return lax.dot_general(a, b, (dims, ((), ())), preferred_element_type=jnp.float32)


def block_kernel(scale, n_own, n_keys, weights, *refs):
    own, keys, outs = refs[: 2 * n_own], refs[2 * n_own : -n_own], refs[-n_own:]
    nt = ((1,), (1,))
    nn = ((1,), (0,))
    img, txt = stacked(own[:n_own]), stacked(own[n_own:])
    key_img, key_txt = stacked(keys[:n_keys]), stacked(keys[n_keys:])
    cross = dot(img, key_txt, nt) - dot(txt, key_img, nt)
    inmodal = dot(img, key_img, nt) - dot(txt, key_txt, nt)
    p_mat = (cross * (weights[0] * scale)).astype(jnp.bfloat16)
    q_mat = (inmodal * (weights[1] * scale)).astype(jnp.bfloat16)
    grad_img = dot(p_mat, key_txt, nn) + dot(q_mat, key_img, nn)
    grad_txt = -dot(p_mat, key_img, nn) - dot(q_mat, key_txt, nn)
    rows = own[0].shape[0]
    for i, out in enumerate(outs):
        out[0] = grad_img[i * rows : (i + 1) * rows]
        out[1] = grad_txt[i * rows : (i + 1) * rows]


def partials(own, keys, weights, scale):
    vmem = pl.BlockSpec(memory_space=pltpu.VMEM)
    smem = pl.BlockSpec(memory_space=pltpu.SMEM)
    n_own, n_keys = len(own[0]), len(keys[0])
    return pl.pallas_call(
        functools.partial(block_kernel, scale, n_own, n_keys),
        out_shape=[jax.ShapeDtypeStruct((2, *x.shape), jnp.float32) for x in own[0]],
        in_specs=[smem] + [vmem] * (2 * n_own + 2 * n_keys),
        out_specs=[vmem] * n_own,
        compiler_params=pltpu.CompilerParams(vmem_limit_bytes=48 * 2**20),
    )(weights, *own[0], *own[1], *keys[0], *keys[1])


def local(images, texts, loss_weights):
    n_row, n_col = lax.axis_size("row"), lax.axis_size("col")
    row_outer, row_inner = halves(n_row)
    col_outer, col_inner = halves(n_col)
    width = images.shape[1]
    batch = images.shape[0] * n_row * n_col
    scale = 1.0 / math.sqrt(width * batch)
    own = (images, texts)

    keys, block = [[images], [texts]], list(own)
    for step in range(col_outer):
        for s in range(2):
            arrived, passed = block[s], []
            if step + 1 < col_outer:
                arrived = lax.ppermute(block[s], "col", outer_ring(n_col))
            for k in range(1, col_inner):
                passed.append(lax.ppermute(block[s], "col", inner_shift(n_col, k)))
            if step + 1 < col_outer:
                arrived, passed = lax.optimization_barrier((arrived, passed))
                block[s] = arrived
                keys[s].append(arrived)
            keys[s] += passed

    column = [[], []]
    for j in range(row_outer):
        first = lax.ppermute(jnp.stack(own), "row", both_shift(n_row, j, 0)) if j else jnp.stack(own)
        for k in range(row_inner):
            pair = lax.ppermute(first, "row", both_shift(n_row, 0, k)) if k else first
            for s in range(2):
                column[s].append(pair[s] if j or k else own[s])

    parts = partials(column, keys, loss_weights, scale)
    sums = []
    for j in reversed(range(row_outer)):
        total = parts[j * row_inner]
        for k in range(1, row_inner):
            total = total + lax.ppermute(parts[j * row_inner + k], "row", inner_shift(n_row, k))
        sums.insert(0, total)
    total = sums[0]
    for j in range(1, row_outer):
        total = total + lax.ppermute(sums[j], "row", outer_shift(n_row, j))
    return total[0], total[1]


def solution(mesh):
    in_specs = (P(("row", "col"), None), P(("row", "col"), None), P())
    out_specs = (P(("row", "col"), None), P(("row", "col"), None))
    return jax.shard_map(local, mesh=mesh, in_specs=in_specs, out_specs=out_specs, check_vma=False)
```

```python
import functools
import math

import jax
import jax.numpy as jnp
from jax import lax
from jax.experimental import pallas as pl
from jax.experimental.pallas import tpu as pltpu
from jax.sharding import PartitionSpec as P

LIMIT = 6.0
TOP = 32768.0


def halves(count):
    inner = 2 if count % 2 == 0 else 1
    return count // inner, inner


def outer_moves(count):
    outer, inner = halves(count)

    def perm(to):
        return [(i, to(i // inner) * inner + i % inner) for i in range(count)]

    moves = []
    if outer & (outer - 1) == 0:
        held, stride = 1, outer // 2
        while stride:
            moves += [(b, perm(lambda o, s=stride: o ^ s)) for b in range(held)]
            held, stride = 2 * held, stride // 2
    else:
        moves = [(0, perm(lambda o, s=s: (o + s) % outer)) for s in range(1, outer)]
    return moves


def inner_shift(count, step):
    _, inner = halves(count)
    return [(i, i // inner * inner + (i + step) % inner) for i in range(count)]


def square_shift(n_row, n_col, j, k):
    r_outer, r_inner = halves(n_row)
    _, c_inner = halves(n_col)
    pairs = []
    for r in range(n_row):
        for c in range(n_col):
            to_r = (r // r_inner + j) % r_outer * r_inner + r % r_inner
            to_c = c // c_inner * c_inner + (c + k) % c_inner
            pairs.append((r * n_col + c, to_r * n_col + to_c))
    return pairs


def stacked(refs, part):
    return jnp.concatenate([ref[part] for ref in refs], axis=0)


def dot(a, b, dims):
    return lax.dot_general(a, b, (dims, ((), ())), preferred_element_type=jnp.float32)


def block_kernel(scale, n_own, n_keys, weights, *refs):
    own, keys = refs[:n_own], refs[n_own : n_own + n_keys]
    mine, unscale, outs = refs[n_own + n_keys], refs[n_own + n_keys + 1], refs[n_own + n_keys + 2 :]
    nt = ((1,), (1,))
    nn = ((1,), (0,))
    img, txt = stacked(own, 0), stacked(own, 1)
    key_img, key_txt = stacked(keys, 0), stacked(keys, 1)
    cross = dot(img, key_txt, nt) - dot(txt, key_img, nt)
    inmodal = dot(img, key_img, nt) - dot(txt, key_txt, nt)
    p_mat = (cross * (weights[0] * scale)).astype(jnp.bfloat16)
    q_mat = (inmodal * (weights[1] * scale)).astype(jnp.bfloat16)
    grad_img = dot(p_mat, key_txt, nn) + dot(q_mat, key_img, nn)
    grad_txt = -dot(p_mat, key_img, nn) - dot(q_mat, key_txt, nn)
    size = jnp.sum(jnp.abs(img.astype(jnp.float32)) + jnp.abs(txt.astype(jnp.float32)), axis=1, keepdims=True)
    count = key_img.shape[0]
    most = size * ((weights[0] + weights[1]) * (1.02 * scale * LIMIT * LIMIT * count)) + 1e-30
    up, down = TOP / most, most / TOP
    rows = own[0].shape[1]
    grad_img, grad_txt = grad_img * up, grad_txt * up
    mine[0] = grad_img[:rows]
    mine[1] = grad_txt[:rows]
    unscale[...] = jnp.broadcast_to(down[:rows], unscale.shape)
    for i, out in enumerate(outs, 1):
        out[0] = grad_img[i * rows : (i + 1) * rows]
        out[1] = grad_txt[i * rows : (i + 1) * rows]


def partials(own, keys, weights, scale):
    vmem = pl.BlockSpec(memory_space=pltpu.VMEM)
    smem = pl.BlockSpec(memory_space=pltpu.SMEM)
    shape = own[0].shape
    out_shape = [jax.ShapeDtypeStruct(shape, jnp.float32), jax.ShapeDtypeStruct((shape[1], 128), jnp.float32)]
    out_shape += [jax.ShapeDtypeStruct(shape, jnp.float32)] * (len(own) - 1)
    return pl.pallas_call(
        functools.partial(block_kernel, scale, len(own), len(keys)),
        out_shape=out_shape,
        in_specs=[smem] + [vmem] * (len(own) + len(keys)),
        out_specs=[vmem] * len(out_shape),
        compiler_params=pltpu.CompilerParams(vmem_limit_bytes=48 * 2**20),
    )(weights, *own, *keys)


def local(images, texts, loss_weights):
    n_row, n_col = lax.axis_size("row"), lax.axis_size("col")
    width = images.shape[1]
    batch = images.shape[0] * n_row * n_col
    scale = 1.0 / math.sqrt(width * batch)
    both = ("row", "col")
    square = [(j, k) for j in range(halves(n_row)[0]) for k in range(halves(n_col)[1])][1:]
    own = jnp.stack([images, texts])

    line = [own]
    for which, perm in outer_moves(n_col):
        line.append(lax.ppermute(line[which], "col", perm))
    keys = list(line)
    for k in range(1, halves(n_row)[1]):
        keys += [lax.ppermute(block, "row", inner_shift(n_row, k)) for block in line]

    rows = [own] + [lax.ppermute(own, both, square_shift(n_row, n_col, j, k)) for j, k in square]

    mine, unscale, *parts = partials(rows, keys, loss_weights, scale)
    back = [
        lax.ppermute(part.astype(jnp.float16), both, square_shift(n_row, n_col, -j, -k))
        for part, (j, k) in zip(parts, square)
    ]
    down = unscale[:, :1]
    grads = []
    for s in range(2):
        total = mine[s]
        for part in back:
            total = total + part[s].astype(jnp.float32)
        grads.append(total * down)
    return tuple(grads)


def solution(mesh):
    in_specs = (P(("row", "col"), None), P(("row", "col"), None), P())
    out_specs = (P(("row", "col"), None), P(("row", "col"), None))
    return jax.shard_map(local, mesh=mesh, in_specs=in_specs, out_specs=out_specs, check_vma=False)
```

```python
import functools
import math

import jax
import jax.numpy as jnp
from jax import lax
from jax.experimental import pallas as pl
from jax.experimental.pallas import tpu as pltpu
from jax.sharding import PartitionSpec as P

LIMIT = 6.0
TOP = 32768.0


def halves(count):
    inner = 2 if count % 2 == 0 else 1
    return count // inner, inner


def outer_moves(count):
    outer, inner = halves(count)

    def perm(to):
        return [(i, to(i // inner) * inner + i % inner) for i in range(count)]

    moves = []
    if outer & (outer - 1) == 0:
        held, stride = 1, outer // 2
        while stride:
            moves += [(b, perm(lambda o, s=stride: o ^ s)) for b in range(held)]
            held, stride = 2 * held, stride // 2
    else:
        moves = [(0, perm(lambda o, s=s: (o + s) % outer)) for s in range(1, outer)]
    return moves


def inner_shift(count, step):
    _, inner = halves(count)
    return [(i, i // inner * inner + (i + step) % inner) for i in range(count)]


def square_shift(n_row, n_col, j, k):
    r_outer, r_inner = halves(n_row)
    _, c_inner = halves(n_col)
    pairs = []
    for r in range(n_row):
        for c in range(n_col):
            to_r = (r // r_inner + j) % r_outer * r_inner + r % r_inner
            to_c = c // c_inner * c_inner + (c + k) % c_inner
            pairs.append((r * n_col + c, to_r * n_col + to_c))
    return pairs


def dot(a, b, dims):
    return lax.dot_general(a, b, (dims, ((), ())), preferred_element_type=jnp.float32)


def join(refs):
    return [jnp.concatenate([ref[s] for ref in refs], axis=0) for s in range(2)]


def products(img, txt, key_img, key_txt, weights, scale):
    n, m = img.shape[0], key_img.shape[0]
    scores = dot(jnp.concatenate([img, txt]), jnp.concatenate([key_img, key_txt]), ((1,), (1,)))
    cross = scores[:n, m:] - scores[n:, :m]
    inmodal = scores[:n, :m] - scores[n:, m:]
    p_mat = (cross * (weights[0] * scale)).astype(jnp.bfloat16)
    q_mat = (inmodal * (weights[1] * scale)).astype(jnp.bfloat16)
    both = jnp.concatenate([p_mat, q_mat], axis=1)
    nn = ((1,), (0,))
    grad_img = dot(both, jnp.concatenate([key_txt, key_img]), nn)
    grad_txt = dot(both, jnp.concatenate([key_img, key_txt]), nn)
    return grad_img, -grad_txt


def early_kernel(scale, total, n, weights, *refs):
    img, txt = join(refs[:n])
    key_img, key_txt = join(refs[n:-3])
    acc, up, down = refs[-3:]
    grad_img, grad_txt = products(img, txt, key_img, key_txt, weights, scale)
    acc[0] = grad_img
    acc[1] = grad_txt
    size = jnp.sum(jnp.abs(img.astype(jnp.float32)) + jnp.abs(txt.astype(jnp.float32)), axis=1, keepdims=True)
    most = size * ((weights[0] + weights[1]) * (1.02 * scale * LIMIT * LIMIT * total)) + 1e-30
    rows = down.shape[0]
    up[...] = jnp.broadcast_to(TOP / most, up.shape)
    down[...] = jnp.broadcast_to((most / TOP)[:rows], down.shape)


def late_kernel(scale, n, weights, *refs):
    img, txt = join(refs[:n])
    key_img, key_txt = join(refs[n : -n - 2])
    acc, up, *outs = refs[-n - 2 :]
    grad_img, grad_txt = products(img, txt, key_img, key_txt, weights, scale)
    factor = up[:, :1]
    grad_img, grad_txt = (grad_img + acc[0]) * factor, (grad_txt + acc[1]) * factor
    rows = outs[0].shape[1]
    for i, out in enumerate(outs):
        out[0] = grad_img[i * rows : (i + 1) * rows]
        out[1] = grad_txt[i * rows : (i + 1) * rows]


def call(kernel, weights, operands, out_shape, flops):
    vmem = pl.BlockSpec(memory_space=pltpu.VMEM)
    smem = pl.BlockSpec(memory_space=pltpu.SMEM)
    moved = sum(x.size * x.dtype.itemsize for x in [*operands, *out_shape])
    return pl.pallas_call(
        kernel,
        out_shape=out_shape,
        in_specs=[smem] + [vmem] * len(operands),
        out_specs=[vmem] * len(out_shape),
        compiler_params=pltpu.CompilerParams(vmem_limit_bytes=40 * 2**20),
        cost_estimate=pl.CostEstimate(flops=flops, bytes_accessed=moved, transcendentals=0),
    )(weights, *operands)


def local(images, texts, loss_weights):
    n_row, n_col = lax.axis_size("row"), lax.axis_size("col")
    row_inner = halves(n_row)[1]
    rows, width = images.shape
    batch = rows * n_row * n_col
    scale = 1.0 / math.sqrt(width * batch)
    both = ("row", "col")
    square = [(j, k) for j in range(halves(n_row)[0]) for k in range(halves(n_col)[1])][1:]
    own = jnp.stack([images, texts])

    mine = [own] + [lax.ppermute(own, both, square_shift(n_row, n_col, j, k)) for j, k in square]

    line = [own]
    for which, perm in outer_moves(n_col):
        line.append(lax.ppermute(line[which], "col", perm))

    def pair(block):
        return [lax.ppermute(block, "row", inner_shift(n_row, k)) for k in range(1, row_inner)]

    early, late = list(line), pair(line[-1])
    for i, block in enumerate(line[:-1]):
        if i < len(square):
            block, mine[i + 1] = lax.optimization_barrier((block, mine[i + 1]))
        early += pair(block)

    total = rows * len(line) * row_inner
    many = rows * len(mine)
    f32 = jnp.float32

    def flops(keys):
        return 16 * many * width * rows * len(keys)

    acc, up, down = call(
        functools.partial(early_kernel, scale, total, len(mine)),
        loss_weights,
        mine + early,
        [jax.ShapeDtypeStruct(s, f32) for s in [(2, many, width), (many, 128), (rows, 128)]],
        flops(early),
    )
    first, *parts = call(
        functools.partial(late_kernel, scale, len(mine)),
        loss_weights,
        mine + late + [acc, up],
        [jax.ShapeDtypeStruct((2, rows, width), f32)] * len(mine),
        flops(late),
    )
    back = [
        lax.ppermute(part.astype(jnp.float16), both, square_shift(n_row, n_col, -j, -k))
        for part, (j, k) in zip(parts, square)
    ]
    grads = []
    for s in range(2):
        total = first[s]
        for part in back:
            total = total + part[s].astype(f32)
        grads.append(total * down[:, :1])
    return tuple(grads)


def solution(mesh):
    in_specs = (P(("row", "col"), None), P(("row", "col"), None), P())
    out_specs = (P(("row", "col"), None), P(("row", "col"), None))
    return jax.shard_map(local, mesh=mesh, in_specs=in_specs, out_specs=out_specs, check_vma=False)
```

```python
import functools
import math

import jax
import jax.numpy as jnp
from jax import lax
from jax.experimental import pallas as pl
from jax.experimental.pallas import tpu as pltpu
from jax.sharding import PartitionSpec as P

LIMIT = 6.0
TOP = 32768.0


def halves(count):
    inner = 2 if count % 2 == 0 else 1
    return count // inner, inner


def outer_moves(count):
    outer, inner = halves(count)

    def perm(to):
        return [(i, to(i // inner) * inner + i % inner) for i in range(count)]

    moves = []
    if outer & (outer - 1) == 0:
        held, stride = 1, outer // 2
        while stride:
            moves += [(b, perm(lambda o, s=stride: o ^ s)) for b in range(held)]
            held, stride = 2 * held, stride // 2
    else:
        moves = [(0, perm(lambda o, s=s: (o + s) % outer)) for s in range(1, outer)]
    return moves


def inner_shift(count, step):
    _, inner = halves(count)
    return [(i, i // inner * inner + (i + step) % inner) for i in range(count)]


def square_shift(n_row, n_col, j, k):
    r_outer, r_inner = halves(n_row)
    _, c_inner = halves(n_col)
    pairs = []
    for r in range(n_row):
        for c in range(n_col):
            to_r = (r // r_inner + j) % r_outer * r_inner + r % r_inner
            to_c = c // c_inner * c_inner + (c + k) % c_inner
            pairs.append((r * n_col + c, to_r * n_col + to_c))
    return pairs


def dot(a, b, dims):
    return lax.dot_general(a, b, (dims, ((), ())), preferred_element_type=jnp.float32)


def join(refs):
    return jnp.concatenate([ref[s] for s in range(2) for ref in refs], axis=0)


def weigh(rows, keys, weights, scale):
    n, m = rows.shape[0] // 2, keys.shape[0] // 2
    scores = dot(rows, keys, ((1,), (1,)))
    cross = scores[:n, m:] - scores[n:, :m]
    inmodal = scores[:n, :m] - scores[n:, m:]
    p_mat = (cross * (weights[0] * scale)).astype(jnp.bfloat16)
    q_mat = (inmodal * (weights[1] * scale)).astype(jnp.bfloat16)
    return p_mat, q_mat


def tiles(width):
    step = 256 if width % 256 == 0 else width
    return [slice(i, i + step) for i in range(0, width, step)]


def tile_grads(p_mat, q_mat, keys, at):
    m = keys.shape[0] // 2
    img, txt = keys[:m, at], keys[m:, at]
    nn = ((1,), (0,))
    grad_img = dot(jnp.concatenate([q_mat, p_mat], axis=1), jnp.concatenate([img, txt]), nn)
    grad_txt = dot(jnp.concatenate([-p_mat, -q_mat], axis=1), jnp.concatenate([img, txt]), nn)
    return grad_img, grad_txt


def early_kernel(scale, total, n, weights, *refs):
    own, acc, up, down = refs[-4:]
    rows = join(refs[:n])
    own[...] = rows
    keys = join(refs[n:-4])
    p_mat, q_mat = weigh(rows, keys, weights, scale)
    for at in tiles(keys.shape[1]):
        acc[0, :, at], acc[1, :, at] = tile_grads(p_mat, q_mat, keys, at)
    size = jnp.sum(jnp.abs(rows.astype(jnp.float32)), axis=1, keepdims=True)
    size = size[: size.shape[0] // 2] + size[size.shape[0] // 2 :]
    most = size * ((weights[0] + weights[1]) * (1.02 * scale * LIMIT * LIMIT * total)) + 1e-30
    up[...] = jnp.broadcast_to(TOP / most, up.shape)
    down[...] = jnp.broadcast_to((most / TOP)[: down.shape[0]], down.shape)


def late_kernel(scale, n, weights, own, acc, up, *refs):
    outs = refs[-n:]
    keys = join(refs[:-n])
    p_mat, q_mat = weigh(own[...], keys, weights, scale)
    rows = outs[0].shape[1]
    for at in tiles(keys.shape[1]):
        for s, grad in enumerate(tile_grads(p_mat, q_mat, keys, at)):
            grad = (grad + acc[s, :, at]) * up[:, :1]
            for i, out in enumerate(outs):
                out[s, :, at] = grad[i * rows : (i + 1) * rows]


def call(kernel, weights, operands, out_shape, flops):
    vmem = pl.BlockSpec(memory_space=pltpu.VMEM)
    smem = pl.BlockSpec(memory_space=pltpu.SMEM)
    moved = sum(x.size * x.dtype.itemsize for x in [*operands, *out_shape])
    return pl.pallas_call(
        kernel,
        out_shape=out_shape,
        in_specs=[smem] + [vmem] * len(operands),
        out_specs=[vmem] * len(out_shape),
        compiler_params=pltpu.CompilerParams(vmem_limit_bytes=40 * 2**20),
        cost_estimate=pl.CostEstimate(flops=flops, bytes_accessed=moved, transcendentals=0),
    )(weights, *operands)


def local(images, texts, loss_weights):
    n_row, n_col = lax.axis_size("row"), lax.axis_size("col")
    row_inner = halves(n_row)[1]
    rows, width = images.shape
    batch = rows * n_row * n_col
    scale = 1.0 / math.sqrt(width * batch)
    both = ("row", "col")
    square = [(j, k) for j in range(halves(n_row)[0]) for k in range(halves(n_col)[1])][1:]
    own = jnp.stack([images, texts])

    mine = [own] + [lax.ppermute(own, both, square_shift(n_row, n_col, j, k)) for j, k in square]

    line = [own]
    for which, perm in outer_moves(n_col):
        line.append(lax.ppermute(line[which], "col", perm))

    def pair(block):
        return [lax.ppermute(block, "row", inner_shift(n_row, k)) for k in range(1, row_inner)]

    early, copies = line[:-1], [copy for block in line[:-1] for copy in pair(block)]
    total = rows * len(line) * row_inner
    many = rows * len(mine)
    f32 = jnp.float32

    def flops(keys):
        return 16 * many * width * rows * len(keys)

    joined, acc, up, down = call(
        functools.partial(early_kernel, scale, total, len(mine)),
        loss_weights,
        mine + early,
        [jax.ShapeDtypeStruct((2 * many, width), images.dtype)]
        + [jax.ShapeDtypeStruct(s, f32) for s in [(2, many, width), (many, 128), (rows, 128)]],
        flops(early),
    )
    last, acc = lax.optimization_barrier((line[-1], acc))
    late = copies + [last] + pair(last)
    first, *parts = call(
        functools.partial(late_kernel, scale, len(mine)),
        loss_weights,
        [joined, acc, up] + late,
        [jax.ShapeDtypeStruct((2, rows, width), f32)] * len(mine),
        flops(late),
    )
    back = [
        lax.ppermute(part.astype(jnp.float16), both, square_shift(n_row, n_col, -j, -k))
        for part, (j, k) in zip(parts, square)
    ]
    grads = []
    for s in range(2):
        total = first[s]
        for part in back:
            total = total + part[s].astype(f32)
        grads.append(total * down[:, :1])
    return tuple(grads)


def solution(mesh):
    in_specs = (P(("row", "col"), None), P(("row", "col"), None), P())
    out_specs = (P(("row", "col"), None), P(("row", "col"), None))
    return jax.shard_map(local, mesh=mesh, in_specs=in_specs, out_specs=out_specs, check_vma=False)
```

```python
import functools
import math

import jax
import jax.numpy as jnp
from jax import lax
from jax.experimental import pallas as pl
from jax.experimental.pallas import tpu as pltpu
from jax.sharding import PartitionSpec as P

LIMIT = 6.0
TOP = 32768.0


def halves(count):
    inner = 2 if count % 2 == 0 else 1
    return count // inner, inner


def outer_moves(count):
    outer, inner = halves(count)

    def perm(to):
        return [(i, to(i // inner) * inner + i % inner) for i in range(count)]

    moves = []
    if outer & (outer - 1) == 0:
        held, stride = 1, outer // 2
        while stride:
            moves += [(b, perm(lambda o, s=stride: o ^ s)) for b in range(held)]
            held, stride = 2 * held, stride // 2
    else:
        moves = [(0, perm(lambda o, s=s: (o + s) % outer)) for s in range(1, outer)]
    return moves


def inner_shift(count, step):
    _, inner = halves(count)
    return [(i, i // inner * inner + (i + step) % inner) for i in range(count)]


def square_shift(n_row, n_col, j, k):
    r_outer, r_inner = halves(n_row)
    _, c_inner = halves(n_col)
    pairs = []
    for r in range(n_row):
        for c in range(n_col):
            to_r = (r // r_inner + j) % r_outer * r_inner + r % r_inner
            to_c = c // c_inner * c_inner + (c + k) % c_inner
            pairs.append((r * n_col + c, to_r * n_col + to_c))
    return pairs


def dot(a, b, dims):
    return lax.dot_general(a, b, (dims, ((), ())), preferred_element_type=jnp.float32)


def join(refs):
    return jnp.concatenate([ref[s] for s in range(2) for ref in refs], axis=0)


def weigh(rows, keys, factors):
    n, m = rows.shape[0] // 2, keys.shape[0] // 2
    scores = dot(rows, keys, ((1,), (1,)))
    cross = scores[:n, m:] - scores[n:, :m]
    inmodal = scores[:n, :m] - scores[n:, m:]
    p_mat = (cross * factors[0:1, 0:1]).astype(jnp.bfloat16)
    q_mat = (inmodal * factors[1:2, 0:1]).astype(jnp.bfloat16)
    return p_mat, q_mat


def tiles(width):
    step = 256 if width % 256 == 0 else width
    return [slice(i, i + step) for i in range(0, width, step)]


def tile_grads(p_mat, q_mat, keys, at):
    m = keys.shape[0] // 2
    img, txt = keys[:m, at], keys[m:, at]
    nn = ((1,), (0,))
    grad_img = dot(jnp.concatenate([q_mat, p_mat], axis=1), jnp.concatenate([img, txt]), nn)
    grad_txt = dot(jnp.concatenate([-p_mat, -q_mat], axis=1), jnp.concatenate([img, txt]), nn)
    return grad_img, grad_txt


def early_kernel(total, n, factors, *refs):
    own, acc, up, down = refs[-4:]
    rows = join(refs[:n])
    own[...] = rows
    keys = join(refs[n:-4])
    p_mat, q_mat = weigh(rows, keys, factors)
    for at in tiles(keys.shape[1]):
        acc[0, :, at], acc[1, :, at] = tile_grads(p_mat, q_mat, keys, at)
    size = jnp.sum(jnp.abs(rows.astype(jnp.float32)), axis=1, keepdims=True)
    size = size[: size.shape[0] // 2] + size[size.shape[0] // 2 :]
    most = size * ((factors[0:1, 0:1] + factors[1:2, 0:1]) * (1.02 * LIMIT * LIMIT * total)) + 1e-30
    up[...] = jnp.broadcast_to(TOP / most, up.shape)
    down[...] = jnp.broadcast_to((most / TOP)[: down.shape[0]], down.shape)


def late_kernel(n, factors, own, acc, up, *refs):
    outs = refs[-n:]
    keys = join(refs[:-n])
    p_mat, q_mat = weigh(own[...], keys, factors)
    rows = outs[0].shape[1]
    for at in tiles(keys.shape[1]):
        for s, grad in enumerate(tile_grads(p_mat, q_mat, keys, at)):
            grad = (grad + acc[s, :, at]) * up[:, :1]
            for i, out in enumerate(outs):
                out[s, :, at] = grad[i * rows : (i + 1) * rows]


def call(kernel, operands, out_shape, flops):
    vmem = pl.BlockSpec(memory_space=pltpu.VMEM)
    moved = sum(x.size * x.dtype.itemsize for x in [*operands, *out_shape])
    return pl.pallas_call(
        kernel,
        out_shape=out_shape,
        in_specs=[vmem] * len(operands),
        out_specs=[vmem] * len(out_shape),
        compiler_params=pltpu.CompilerParams(vmem_limit_bytes=40 * 2**20),
        cost_estimate=pl.CostEstimate(flops=flops, bytes_accessed=moved, transcendentals=0),
    )(*operands)


def local(images, texts, loss_weights):
    n_row, n_col = lax.axis_size("row"), lax.axis_size("col")
    row_inner = halves(n_row)[1]
    rows, width = images.shape
    batch = rows * n_row * n_col
    factors = jnp.broadcast_to((loss_weights * (1.0 / math.sqrt(width * batch)))[:, None], (2, 128))
    both = ("row", "col")
    square = [(j, k) for j in range(halves(n_row)[0]) for k in range(halves(n_col)[1])][1:]
    own = jnp.stack([images, texts])

    mine = [own] + [lax.ppermute(own, both, square_shift(n_row, n_col, j, k)) for j, k in square]

    line = [own]
    for which, perm in outer_moves(n_col):
        line.append(lax.ppermute(line[which], "col", perm))

    def pair(block):
        return [lax.ppermute(block, "row", inner_shift(n_row, k)) for k in range(1, row_inner)]

    early, copies = line[:-1], [copy for block in line[:-1] for copy in pair(block)]
    total = rows * len(line) * row_inner
    many = rows * len(mine)
    f32 = jnp.float32

    def flops(keys):
        return 16 * many * width * rows * len(keys)

    joined, acc, up, down = call(
        functools.partial(early_kernel, total, len(mine)),
        [factors] + mine + early,
        [jax.ShapeDtypeStruct((2 * many, width), images.dtype)]
        + [jax.ShapeDtypeStruct(s, f32) for s in [(2, many, width), (many, 128), (rows, 128)]],
        flops(early),
    )
    last, acc = lax.optimization_barrier((line[-1], acc))
    late = copies + [last] + pair(last)
    first, *parts = call(
        functools.partial(late_kernel, len(mine)),
        [factors, joined, acc, up] + late,
        [jax.ShapeDtypeStruct((2, rows, width), f32)] * len(mine),
        flops(late),
    )
    back = [
        lax.ppermute(part.astype(jnp.float16), both, square_shift(n_row, n_col, -j, -k))
        for part, (j, k) in zip(parts, square)
    ]
    grads = []
    for s in range(2):
        total = first[s]
        for part in back:
            total = total + part[s].astype(f32)
        grads.append(total * down[:, :1])
    return tuple(grads)


def solution(mesh):
    in_specs = (P(("row", "col"), None), P(("row", "col"), None), P())
    out_specs = (P(("row", "col"), None), P(("row", "col"), None))
    return jax.shard_map(local, mesh=mesh, in_specs=in_specs, out_specs=out_specs, check_vma=False)
```

```python
import functools
import math

import jax
import jax.numpy as jnp
from jax import lax
from jax.experimental import pallas as pl
from jax.experimental.pallas import tpu as pltpu
from jax.sharding import PartitionSpec as P

LIMIT = 6.0
TOP = 32768.0


def halves(count):
    inner = 2 if count % 2 == 0 else 1
    return count // inner, inner


def outer_moves(count):
    outer, inner = halves(count)

    def perm(to):
        return [(i, to(i // inner) * inner + i % inner) for i in range(count)]

    moves = []
    if outer & (outer - 1) == 0:
        held, stride = 1, outer // 2
        while stride:
            moves += [(b, perm(lambda o, s=stride: o ^ s)) for b in range(held)]
            held, stride = 2 * held, stride // 2
    else:
        moves = [(0, perm(lambda o, s=s: (o + s) % outer)) for s in range(1, outer)]
    return moves


def inner_shift(count, step):
    _, inner = halves(count)
    return [(i, i // inner * inner + (i + step) % inner) for i in range(count)]


def square_shift(n_row, n_col, j, k):
    r_outer, r_inner = halves(n_row)
    _, c_inner = halves(n_col)
    pairs = []
    for r in range(n_row):
        for c in range(n_col):
            to_r = (r // r_inner + j) % r_outer * r_inner + r % r_inner
            to_c = c // c_inner * c_inner + (c + k) % c_inner
            pairs.append((r * n_col + c, to_r * n_col + to_c))
    return pairs


def dot(a, b, dims):
    return lax.dot_general(a, b, (dims, ((), ())), preferred_element_type=jnp.float32)


def join(refs):
    return jnp.concatenate([ref[s] for s in range(2) for ref in refs], axis=0)


def weigh(rows, keys, factors):
    n, m = rows.shape[0] // 2, keys.shape[0] // 2
    scores = dot(rows, keys, ((1,), (1,)))
    cross = scores[:n, m:] - scores[n:, :m]
    inmodal = scores[:n, :m] - scores[n:, m:]
    p_mat = (cross * factors[0:1, 0:1]).astype(jnp.bfloat16)
    q_mat = (inmodal * factors[1:2, 0:1]).astype(jnp.bfloat16)
    return p_mat, q_mat


def tiles(width):
    step = 256 if width % 256 == 0 else width
    return [slice(i, i + step) for i in range(0, width, step)]


def tile_grads(p_mat, q_mat, keys, at):
    m = keys.shape[0] // 2
    img, txt = keys[:m, at], keys[m:, at]
    nn = ((1,), (0,))
    grad_img = dot(jnp.concatenate([q_mat, p_mat], axis=1), jnp.concatenate([img, txt]), nn)
    grad_txt = dot(jnp.concatenate([-p_mat, -q_mat], axis=1), jnp.concatenate([img, txt]), nn)
    return grad_img, grad_txt


def early_kernel(total, n, factors, *refs):
    own, acc, up, down = refs[-4:]
    rows = join(refs[:n])
    own[...] = rows
    keys = join(refs[n:-4])
    p_mat, q_mat = weigh(rows, keys, factors)
    for at in tiles(keys.shape[1]):
        acc[0, :, at], acc[1, :, at] = tile_grads(p_mat, q_mat, keys, at)
    size = jnp.sum(jnp.abs(rows.astype(jnp.float32)), axis=1, keepdims=True)
    size = size[: size.shape[0] // 2] + size[size.shape[0] // 2 :]
    most = size * ((factors[0:1, 0:1] + factors[1:2, 0:1]) * (1.02 * LIMIT * LIMIT * total)) + 1e-30
    up[...] = jnp.broadcast_to(TOP / most, up.shape)
    down[...] = jnp.broadcast_to((most / TOP)[: down.shape[0]], down.shape)


def late_kernel(n, factors, own, acc, up, *refs):
    outs = refs[-n:]
    keys = join(refs[:-n])
    p_mat, q_mat = weigh(own[...], keys, factors)
    rows = outs[0].shape[1]
    for at in tiles(keys.shape[1]):
        for s, grad in enumerate(tile_grads(p_mat, q_mat, keys, at)):
            grad = (grad + acc[s, :, at]) * up[:, :1]
            for i, out in enumerate(outs):
                out[s, :, at] = grad[i * rows : (i + 1) * rows]


def call(kernel, operands, out_shape, flops):
    vmem = pl.BlockSpec(memory_space=pltpu.VMEM)
    moved = sum(x.size * x.dtype.itemsize for x in [*operands, *out_shape])
    return pl.pallas_call(
        kernel,
        out_shape=out_shape,
        in_specs=[vmem] * len(operands),
        out_specs=[vmem] * len(out_shape),
        compiler_params=pltpu.CompilerParams(vmem_limit_bytes=40 * 2**20),
        cost_estimate=pl.CostEstimate(flops=flops, bytes_accessed=moved, transcendentals=0),
    )(*operands)


def local(images, texts, loss_weights):
    n_row, n_col = lax.axis_size("row"), lax.axis_size("col")
    row_inner = halves(n_row)[1]
    rows, width = images.shape
    batch = rows * n_row * n_col
    factors = jnp.broadcast_to((loss_weights * (1.0 / math.sqrt(width * batch)))[:, None], (2, 128))
    both = ("row", "col")
    square = [(j, k) for j in range(halves(n_row)[0]) for k in range(halves(n_col)[1])][1:]
    own = jnp.stack([images, texts])

    mine = [own] + [lax.ppermute(own, both, square_shift(n_row, n_col, j, k)) for j, k in square]

    line, apart = [own], {0: [images, texts]}
    for step, (which, perm) in enumerate(outer_moves(n_col), 1):
        if which in apart and (which or step == 1):
            apart[step] = [lax.ppermute(half, "col", perm) for half in apart[which]]
            line.append(jnp.stack(apart[step]))
        else:
            line.append(lax.ppermute(line[which], "col", perm))

    def pair(block):
        return [lax.ppermute(block, "row", inner_shift(n_row, k)) for k in range(1, row_inner)]

    early, copies = line[:-1], []
    for i, block in enumerate(line[:-1]):
        if i == 0 and square:
            block, mine[-2] = lax.optimization_barrier((block, mine[-2]))
        copies += pair(block)
    total = rows * len(line) * row_inner
    many = rows * len(mine)
    f32 = jnp.float32

    def flops(keys):
        return 16 * many * width * rows * len(keys)

    joined, acc, up, down = call(
        functools.partial(early_kernel, total, len(mine)),
        [factors] + mine + early,
        [jax.ShapeDtypeStruct((2 * many, width), images.dtype)]
        + [jax.ShapeDtypeStruct(s, f32) for s in [(2, many, width), (many, 128), (rows, 128)]],
        flops(early),
    )
    last, acc = lax.optimization_barrier((line[-1], acc))
    late = copies + [last] + pair(last)
    first, *parts = call(
        functools.partial(late_kernel, len(mine)),
        [factors, joined, acc, up] + late,
        [jax.ShapeDtypeStruct((2, rows, width), f32)] * len(mine),
        flops(late),
    )
    back = [
        lax.ppermute(part.astype(jnp.float16), both, square_shift(n_row, n_col, -j, -k))
        for part, (j, k) in zip(parts, square)
    ]
    grads = []
    for s in range(2):
        total = first[s]
        for part in back:
            total = total + part[s].astype(f32)
        grads.append(total * down[:, :1])
    return tuple(grads)


def solution(mesh):
    in_specs = (P(("row", "col"), None), P(("row", "col"), None), P())
    out_specs = (P(("row", "col"), None), P(("row", "col"), None))
    return jax.shard_map(local, mesh=mesh, in_specs=in_specs, out_specs=out_specs, check_vma=False)
```

```python
import functools
import math

import jax
import jax.numpy as jnp
from jax import lax
from jax.experimental import pallas as pl
from jax.experimental.pallas import tpu as pltpu
from jax.sharding import PartitionSpec as P

LIMIT = 6.0
TOP = 32768.0


def halves(count):
    inner = 2 if count % 2 == 0 else 1
    return count // inner, inner


def outer_moves(count):
    outer, inner = halves(count)

    def perm(to):
        return [(i, to(i // inner) * inner + i % inner) for i in range(count)]

    moves = []
    if outer & (outer - 1) == 0:
        held, stride = 1, outer // 2
        while stride:
            moves += [(b, perm(lambda o, s=stride: o ^ s)) for b in range(held)]
            held, stride = 2 * held, stride // 2
    else:
        moves = [(0, perm(lambda o, s=s: (o + s) % outer)) for s in range(1, outer)]
    return moves


def inner_shift(count, step):
    _, inner = halves(count)
    return [(i, i // inner * inner + (i + step) % inner) for i in range(count)]


def square_shift(n_row, n_col, j, k):
    r_outer, r_inner = halves(n_row)
    _, c_inner = halves(n_col)
    pairs = []
    for r in range(n_row):
        for c in range(n_col):
            to_r = (r // r_inner + j) % r_outer * r_inner + r % r_inner
            to_c = c // c_inner * c_inner + (c + k) % c_inner
            pairs.append((r * n_col + c, to_r * n_col + to_c))
    return pairs


def dot(a, b, dims):
    return lax.dot_general(a, b, (dims, ((), ())), preferred_element_type=jnp.float32)


def join(refs):
    return jnp.concatenate([ref[s] for s in range(2) for ref in refs], axis=0)


def weigh(rows, keys, factors):
    n, m = rows.shape[0] // 2, keys.shape[0] // 2
    scores = dot(rows, keys, ((1,), (1,)))
    cross = scores[:n, m:] - scores[n:, :m]
    inmodal = scores[:n, :m] - scores[n:, m:]
    p_mat = (cross * factors[0:1, 0:1]).astype(jnp.bfloat16)
    q_mat = (inmodal * factors[1:2, 0:1]).astype(jnp.bfloat16)
    return p_mat, q_mat


def tiles(width):
    step = 256 if width % 256 == 0 else width
    return [slice(i, i + step) for i in range(0, width, step)]


def tile_grads(p_mat, q_mat, keys, at):
    m = keys.shape[0] // 2
    img, txt = keys[:m, at], keys[m:, at]
    nn = ((1,), (0,))
    grad_img = dot(jnp.concatenate([q_mat, p_mat], axis=1), jnp.concatenate([img, txt]), nn)
    grad_txt = dot(jnp.concatenate([-p_mat, -q_mat], axis=1), jnp.concatenate([img, txt]), nn)
    return grad_img, grad_txt


def early_kernel(total, n, factors, *refs):
    own, acc, up, down = refs[-4:]
    rows = join(refs[:n])
    own[...] = rows
    keys = join(refs[n:-4])
    p_mat, q_mat = weigh(rows, keys, factors)
    for at in tiles(keys.shape[1]):
        acc[0, :, at], acc[1, :, at] = tile_grads(p_mat, q_mat, keys, at)
    size = jnp.sum(jnp.abs(rows.astype(jnp.float32)), axis=1, keepdims=True)
    size = size[: size.shape[0] // 2] + size[size.shape[0] // 2 :]
    most = size * ((factors[0:1, 0:1] + factors[1:2, 0:1]) * (1.02 * LIMIT * LIMIT * total)) + 1e-30
    up[...] = jnp.broadcast_to(TOP / most, up.shape)
    down[...] = jnp.broadcast_to((most / TOP)[: down.shape[0]], down.shape)


def late_kernel(n, factors, own, acc, up, *refs):
    outs = refs[-n:]
    keys = join(refs[:-n])
    p_mat, q_mat = weigh(own[...], keys, factors)
    rows = outs[0].shape[1]
    for at in tiles(keys.shape[1]):
        for s, grad in enumerate(tile_grads(p_mat, q_mat, keys, at)):
            grad = (grad + acc[s, :, at]) * up[:, :1]
            for i, out in enumerate(outs):
                out[s, :, at] = grad[i * rows : (i + 1) * rows]


def stack_kernel(images, texts, out, sems):
    copies = [pltpu.make_async_copy(x, out.at[i], sems.at[i]) for i, x in enumerate((images, texts))]
    for copy in copies:
        copy.start()
    for copy in copies:
        copy.wait()


def stack(images, texts):
    return pl.pallas_call(
        stack_kernel,
        out_shape=jax.ShapeDtypeStruct((2, *images.shape), images.dtype),
        in_specs=[pl.BlockSpec(memory_space=pltpu.HBM)] * 2,
        out_specs=pl.BlockSpec(memory_space=pltpu.VMEM),
        scratch_shapes=[pltpu.SemaphoreType.DMA((2,))],
        compiler_params=pltpu.CompilerParams(vmem_limit_bytes=62 * 2**20),
    )(images, texts)


def call(kernel, operands, out_shape, flops):
    vmem = pl.BlockSpec(memory_space=pltpu.VMEM)
    moved = sum(x.size * x.dtype.itemsize for x in [*operands, *out_shape])
    return pl.pallas_call(
        kernel,
        out_shape=out_shape,
        in_specs=[vmem] * len(operands),
        out_specs=[vmem] * len(out_shape),
        compiler_params=pltpu.CompilerParams(vmem_limit_bytes=40 * 2**20),
        cost_estimate=pl.CostEstimate(flops=flops, bytes_accessed=moved, transcendentals=0),
    )(*operands)


def local(images, texts, loss_weights):
    n_row, n_col = lax.axis_size("row"), lax.axis_size("col")
    row_inner = halves(n_row)[1]
    rows, width = images.shape
    batch = rows * n_row * n_col
    factors = jnp.broadcast_to((loss_weights * (1.0 / math.sqrt(width * batch)))[:, None], (2, 128))
    both = ("row", "col")
    square = [(j, k) for j in range(halves(n_row)[0]) for k in range(halves(n_col)[1])][1:]
    own = stack(images, texts)

    mine = [own] + [lax.ppermute(own, both, square_shift(n_row, n_col, j, k)) for j, k in square]

    line = [own]
    for which, perm in outer_moves(n_col):
        line.append(lax.ppermute(line[which], "col", perm))

    def pair(block):
        return [lax.ppermute(block, "row", inner_shift(n_row, k)) for k in range(1, row_inner)]

    early, copies = line[:-1], [copy for block in line[:-1] for copy in pair(block)]
    total = rows * len(line) * row_inner
    many = rows * len(mine)
    f32 = jnp.float32

    def flops(keys):
        return 16 * many * width * rows * len(keys)

    joined, acc, up, down = call(
        functools.partial(early_kernel, total, len(mine)),
        [factors] + mine + early,
        [jax.ShapeDtypeStruct((2 * many, width), images.dtype)]
        + [jax.ShapeDtypeStruct(s, f32) for s in [(2, many, width), (many, 128), (rows, 128)]],
        flops(early),
    )
    last, acc = lax.optimization_barrier((line[-1], acc))
    late = copies + [last] + pair(last)
    first, *parts = call(
        functools.partial(late_kernel, len(mine)),
        [factors, joined, acc, up] + late,
        [jax.ShapeDtypeStruct((2, rows, width), f32)] * len(mine),
        flops(late),
    )
    back = [
        lax.ppermute(part.astype(jnp.float16), both, square_shift(n_row, n_col, -j, -k))
        for part, (j, k) in reversed(list(zip(parts, square)))
    ]
    grads = []
    for s in range(2):
        total = first[s]
        for part in back:
            total = total + part[s].astype(f32)
        grads.append(total * down[:, :1])
    return tuple(grads)


def solution(mesh):
    in_specs = (P(("row", "col"), None), P(("row", "col"), None), P())
    out_specs = (P(("row", "col"), None), P(("row", "col"), None))
    return jax.shard_map(local, mesh=mesh, in_specs=in_specs, out_specs=out_specs, check_vma=False)
```

```python
import functools
import math

import jax
import jax.numpy as jnp
from jax import lax
from jax.experimental import pallas as pl
from jax.experimental.pallas import tpu as pltpu
from jax.sharding import PartitionSpec as P

LIMIT = 6.0
TOP = 32768.0


def halves(count):
    inner = 2 if count % 2 == 0 else 1
    return count // inner, inner


def outer_moves(count):
    outer, inner = halves(count)

    def perm(to):
        return [(i, to(i // inner) * inner + i % inner) for i in range(count)]

    moves = []
    if outer & (outer - 1) == 0:
        held, stride = 1, outer // 2
        while stride:
            moves += [(b, perm(lambda o, s=stride: o ^ s)) for b in range(held)]
            held, stride = 2 * held, stride // 2
    else:
        moves = [(0, perm(lambda o, s=s: (o + s) % outer)) for s in range(1, outer)]
    return moves


def inner_shift(count, step):
    _, inner = halves(count)
    return [(i, i // inner * inner + (i + step) % inner) for i in range(count)]


def square_shift(n_row, n_col, j, k):
    r_outer, r_inner = halves(n_row)
    _, c_inner = halves(n_col)
    pairs = []
    for r in range(n_row):
        for c in range(n_col):
            to_r = (r // r_inner + j) % r_outer * r_inner + r % r_inner
            to_c = c // c_inner * c_inner + (c + k) % c_inner
            pairs.append((r * n_col + c, to_r * n_col + to_c))
    return pairs


def dot(a, b, dims):
    return lax.dot_general(a, b, (dims, ((), ())), preferred_element_type=jnp.float32)


def join(refs):
    return jnp.concatenate([ref[s] for s in range(2) for ref in refs], axis=0)


def weigh(rows, keys, factors):
    n, m = rows.shape[0] // 2, keys.shape[0] // 2
    scores = dot(rows, keys, ((1,), (1,)))
    cross = scores[:n, m:] - scores[n:, :m]
    inmodal = scores[:n, :m] - scores[n:, m:]
    p_mat = (cross * factors[0:1, 0:1]).astype(jnp.bfloat16)
    q_mat = (inmodal * factors[1:2, 0:1]).astype(jnp.bfloat16)
    return p_mat, q_mat


def tiles(width):
    step = 256 if width % 256 == 0 else width
    return [slice(i, i + step) for i in range(0, width, step)]


def spread(p_mat, q_mat):
    return jnp.concatenate(
        [jnp.concatenate([q_mat, p_mat], axis=1), jnp.concatenate([-p_mat, -q_mat], axis=1)], axis=0
    )


def early_kernel(total, n, factors, *refs):
    own, acc, up, down = refs[-4:]
    rows = join(refs[:n])
    own[...] = rows
    keys = join(refs[n:-4])
    mix = spread(*weigh(rows, keys, factors))
    for at in tiles(keys.shape[1]):
        acc[:, at] = dot(mix, keys[:, at], ((1,), (0,)))
    size = jnp.sum(jnp.abs(rows.astype(jnp.float32)), axis=1, keepdims=True)
    half = size.shape[0] // 2
    size = size[:half] + size[half:]
    most = size * ((factors[0:1, 0:1] + factors[1:2, 0:1]) * (1.02 * LIMIT * LIMIT * total)) + 1e-30
    for s in range(2):
        up[s * half : (s + 1) * half] = jnp.broadcast_to(TOP / most, (half, up.shape[1]))
    down[...] = jnp.broadcast_to((most / TOP)[: down.shape[0]], down.shape)


def member(n_row, n_col, j=0, k=0):
    (r_outer, r_inner), (_, c_inner) = halves(n_row), halves(n_col)
    at_row, at_col = lax.axis_index("row") // r_inner, lax.axis_index("col") % c_inner
    return (at_row + r_outer - j) % r_outer * c_inner + (at_col + c_inner - k) % c_inner


def squares(n_row, n_col):
    (r_outer, r_inner), (c_outer, c_inner) = halves(n_row), halves(n_col)
    return [
        [(j * r_inner + r) * n_col + c * c_inner + k for j in range(r_outer) for k in range(c_inner)]
        for r in range(r_inner)
        for c in range(c_outer)
    ]


def late_kernel(places, factors, own, acc, up, *refs):
    out = refs[-1]
    n = out.shape[0]
    keys = join(refs[:-1])
    slots = [place() for place in places]
    mix = spread(*weigh(own[...], keys, factors))
    rows = out.shape[2]
    for at in tiles(keys.shape[1]):
        grad = (dot(mix, keys[:, at], ((1,), (0,))) + acc[:, at]) * up[:, :1]
        for s in range(2):
            for i, slot in enumerate(slots):
                out[slot, s, :, at] = grad[(s * n + i) * rows : (s * n + i + 1) * rows]


def call(kernel, operands, out_shape, flops):
    vmem = pl.BlockSpec(memory_space=pltpu.VMEM)
    moved = sum(x.size * x.dtype.itemsize for x in [*operands, *out_shape])
    return pl.pallas_call(
        kernel,
        out_shape=out_shape,
        in_specs=[vmem] * len(operands),
        out_specs=[vmem] * len(out_shape),
        compiler_params=pltpu.CompilerParams(vmem_limit_bytes=40 * 2**20),
        cost_estimate=pl.CostEstimate(flops=flops, bytes_accessed=moved, transcendentals=0),
    )(*operands)


def local(images, texts, loss_weights):
    n_row, n_col = lax.axis_size("row"), lax.axis_size("col")
    row_inner = halves(n_row)[1]
    rows, width = images.shape
    batch = rows * n_row * n_col
    factors = jnp.broadcast_to((loss_weights * (1.0 / math.sqrt(width * batch)))[:, None], (2, 128))
    both = ("row", "col")
    square = [(j, k) for j in range(halves(n_row)[0]) for k in range(halves(n_col)[1])][1:]
    own = jnp.stack([images, texts])

    mine = [own] + [lax.ppermute(own, both, square_shift(n_row, n_col, j, k)) for j, k in square]

    line = [own]
    for which, perm in outer_moves(n_col):
        line.append(lax.ppermute(line[which], "col", perm))

    def pair(block):
        return [lax.ppermute(block, "row", inner_shift(n_row, k)) for k in range(1, row_inner)]

    early, copies = line[:-1], [copy for block in line[:-1] for copy in pair(block)]
    total = rows * len(line) * row_inner
    many = rows * len(mine)
    f32 = jnp.float32

    def flops(keys):
        return 16 * many * width * rows * len(keys)

    joined, acc, up, down = call(
        functools.partial(early_kernel, total, len(mine)),
        [factors] + mine + early,
        [jax.ShapeDtypeStruct((2 * many, width), images.dtype)]
        + [jax.ShapeDtypeStruct(s, f32) for s in [(2 * many, width), (2 * many, 128), (rows, 128)]],
        flops(early),
    )
    last, acc = lax.optimization_barrier((line[-1], acc))
    late = copies + [last] + pair(last)
    places = [functools.partial(member, n_row, n_col, j, k) for j, k in [(0, 0), *square]]
    (parts,) = call(
        functools.partial(late_kernel, places),
        [factors, joined, acc, up] + late,
        [jax.ShapeDtypeStruct((len(mine), 2, rows, width), f32)],
        flops(late),
    )
    back = lax.all_to_all(parts.astype(jnp.float16), both, 0, 0, axis_index_groups=squares(n_row, n_col))
    grads = []
    for s in range(2):
        total = back[0, s].astype(f32)
        for i in range(1, len(mine)):
            total = total + back[i, s].astype(f32)
        grads.append(total * down[:, :1])
    return tuple(grads)


def solution(mesh):
    in_specs = (P(("row", "col"), None), P(("row", "col"), None), P())
    out_specs = (P(("row", "col"), None), P(("row", "col"), None))
    return jax.shard_map(local, mesh=mesh, in_specs=in_specs, out_specs=out_specs, check_vma=False)
```

```python
import functools
import math

import jax
import jax.numpy as jnp
from jax import lax
from jax.experimental import pallas as pl
from jax.experimental.pallas import tpu as pltpu
from jax.sharding import PartitionSpec as P

LIMIT = 6.0
TOP = 32768.0


def halves(count):
    inner = 2 if count % 2 == 0 else 1
    return count // inner, inner


def outer_moves(count):
    outer, inner = halves(count)

    def perm(to):
        return [(i, to(i // inner) * inner + i % inner) for i in range(count)]

    moves = []
    if outer & (outer - 1) == 0:
        held, stride = 1, outer // 2
        while stride:
            moves += [(b, perm(lambda o, s=stride: o ^ s)) for b in range(held)]
            held, stride = 2 * held, stride // 2
    else:
        moves = [(0, perm(lambda o, s=s: (o + s) % outer)) for s in range(1, outer)]
    return moves


def inner_shift(count, step):
    _, inner = halves(count)
    return [(i, i // inner * inner + (i + step) % inner) for i in range(count)]


def square_shift(n_row, n_col, j, k):
    r_outer, r_inner = halves(n_row)
    _, c_inner = halves(n_col)
    pairs = []
    for r in range(n_row):
        for c in range(n_col):
            to_r = (r // r_inner + j) % r_outer * r_inner + r % r_inner
            to_c = c // c_inner * c_inner + (c + k) % c_inner
            pairs.append((r * n_col + c, to_r * n_col + to_c))
    return pairs


def dot(a, b, dims):
    return lax.dot_general(a, b, (dims, ((), ())), preferred_element_type=jnp.float32)


def join(refs):
    return jnp.concatenate([ref[s] for s in range(2) for ref in refs], axis=0)


def weigh(rows, keys, factors):
    n, m = rows.shape[0] // 2, keys.shape[0] // 2
    scores = dot(rows, keys, ((1,), (1,)))
    cross = scores[:n, m:] - scores[n:, :m]
    inmodal = scores[:n, :m] - scores[n:, m:]
    p_mat = (cross * factors[0:1, 0:1]).astype(jnp.bfloat16)
    q_mat = (inmodal * factors[1:2, 0:1]).astype(jnp.bfloat16)
    return p_mat, q_mat


def tiles(width):
    step = 256 if width % 256 == 0 else width
    return [slice(i, i + step) for i in range(0, width, step)]


def tile_grads(p_mat, q_mat, keys, at):
    m = keys.shape[0] // 2
    img, txt = keys[:m, at], keys[m:, at]
    nn = ((1,), (0,))
    grad_img = dot(jnp.concatenate([q_mat, p_mat], axis=1), jnp.concatenate([img, txt]), nn)
    grad_txt = dot(jnp.concatenate([-p_mat, -q_mat], axis=1), jnp.concatenate([img, txt]), nn)
    return grad_img, grad_txt


def early_kernel(total, n, factors, *refs):
    own, acc, up, down = refs[-4:]
    rows = join(refs[:n])
    own[...] = rows
    keys = join(refs[n:-4])
    p_mat, q_mat = weigh(rows, keys, factors)
    for at in tiles(keys.shape[1]):
        acc[0, :, at], acc[1, :, at] = tile_grads(p_mat, q_mat, keys, at)
    size = jnp.sum(jnp.abs(rows.astype(jnp.float32)), axis=1, keepdims=True)
    size = size[: size.shape[0] // 2] + size[size.shape[0] // 2 :]
    most = size * ((factors[0:1, 0:1] + factors[1:2, 0:1]) * (1.02 * LIMIT * LIMIT * total)) + 1e-30
    up[...] = jnp.broadcast_to(TOP / most, up.shape)
    down[...] = jnp.broadcast_to((most / TOP)[: down.shape[0]], down.shape)


def late_kernel(first, factors, own, acc, up, *refs, count):
    outs = refs[-count:]
    keys = join(refs[:-count])
    rows, many = outs[0].shape[1], own.shape[0] // 2
    low, size = first * rows, count * rows
    mine = jnp.concatenate([own[low : low + size], own[many + low : many + low + size]], axis=0)
    p_mat, q_mat = weigh(mine, keys, factors)
    for at in tiles(keys.shape[1]):
        for s, grad in enumerate(tile_grads(p_mat, q_mat, keys, at)):
            grad = (grad + acc[s, low : low + size, at]) * up[low : low + size, :1]
            for i, out in enumerate(outs):
                out[s, :, at] = grad[i * rows : (i + 1) * rows]


def call(kernel, operands, out_shape, flops):
    vmem = pl.BlockSpec(memory_space=pltpu.VMEM)
    moved = sum(x.size * x.dtype.itemsize for x in [*operands, *out_shape])
    return pl.pallas_call(
        kernel,
        out_shape=out_shape,
        in_specs=[vmem] * len(operands),
        out_specs=[vmem] * len(out_shape),
        compiler_params=pltpu.CompilerParams(vmem_limit_bytes=40 * 2**20),
        cost_estimate=pl.CostEstimate(flops=flops, bytes_accessed=moved, transcendentals=0),
    )(*operands)


def local(images, texts, loss_weights):
    n_row, n_col = lax.axis_size("row"), lax.axis_size("col")
    row_inner = halves(n_row)[1]
    rows, width = images.shape
    batch = rows * n_row * n_col
    factors = jnp.broadcast_to((loss_weights * (1.0 / math.sqrt(width * batch)))[:, None], (2, 128))
    both = ("row", "col")
    square = [(j, k) for j in range(halves(n_row)[0]) for k in range(halves(n_col)[1])][1:]
    own = jnp.stack([images, texts])

    mine = [own] + [lax.ppermute(own, both, square_shift(n_row, n_col, j, k)) for j, k in square]

    line = [own]
    for which, perm in outer_moves(n_col):
        line.append(lax.ppermute(line[which], "col", perm))

    def pair(block):
        return [lax.ppermute(block, "row", inner_shift(n_row, k)) for k in range(1, row_inner)]

    early, copies = line[:-1], [copy for block in line[:-1] for copy in pair(block)]
    total = rows * len(line) * row_inner
    many = rows * len(mine)
    f32 = jnp.float32

    def flops(keys):
        return 16 * many * width * rows * len(keys)

    joined, acc, up, down = call(
        functools.partial(early_kernel, total, len(mine)),
        [factors] + mine + early,
        [jax.ShapeDtypeStruct((2 * many, width), images.dtype)]
        + [jax.ShapeDtypeStruct(s, f32) for s in [(2, many, width), (many, 128), (rows, 128)]],
        flops(early),
    )
    last, acc = lax.optimization_barrier((line[-1], acc))
    late = copies + [last] + pair(last)
    def late_call(first, count):
        return call(
            functools.partial(late_kernel, first, count=count),
            [factors, joined, acc, up] + late,
            [jax.ShapeDtypeStruct((2, rows, width), f32)] * count,
            flops(late) * count // len(mine),
        )

    parts = late_call(len(mine) - 1, 1)
    if len(mine) > 1:
        parts = late_call(0, len(mine) - 1) + parts
    back = [
        lax.ppermute(part.astype(jnp.float16), both, square_shift(n_row, n_col, -j, -k))
        for part, (j, k) in zip(parts[1:], square)
    ]
    grads = []
    for s in range(2):
        total = parts[0][s]
        for part in back:
            total = total + part[s].astype(f32)
        grads.append(total * down[:, :1])
    return tuple(grads)


def solution(mesh):
    in_specs = (P(("row", "col"), None), P(("row", "col"), None), P())
    out_specs = (P(("row", "col"), None), P(("row", "col"), None))
    return jax.shard_map(local, mesh=mesh, in_specs=in_specs, out_specs=out_specs, check_vma=False)
```

```python
import functools
import math

import jax
import jax.numpy as jnp
from jax import lax
from jax.experimental import pallas as pl
from jax.experimental.pallas import tpu as pltpu
from jax.sharding import PartitionSpec as P

LIMIT = 6.0
TOP = 32768.0


def halves(count):
    inner = 2 if count % 2 == 0 else 1
    return count // inner, inner


def outer_moves(count):
    outer, inner = halves(count)

    def perm(to):
        return [(i, to(i // inner) * inner + i % inner) for i in range(count)]

    moves = []
    if outer & (outer - 1) == 0:
        held, stride = 1, outer // 2
        while stride:
            moves += [(b, perm(lambda o, s=stride: o ^ s)) for b in range(held)]
            held, stride = 2 * held, stride // 2
    else:
        moves = [(0, perm(lambda o, s=s: (o + s) % outer)) for s in range(1, outer)]
    return moves


def inner_shift(count, step):
    _, inner = halves(count)
    return [(i, i // inner * inner + (i + step) % inner) for i in range(count)]


def square_shift(n_row, n_col, j, k):
    r_outer, r_inner = halves(n_row)
    _, c_inner = halves(n_col)
    pairs = []
    for r in range(n_row):
        for c in range(n_col):
            to_r = (r // r_inner + j) % r_outer * r_inner + r % r_inner
            to_c = c // c_inner * c_inner + (c + k) % c_inner
            pairs.append((r * n_col + c, to_r * n_col + to_c))
    return pairs


def dot(a, b, dims):
    return lax.dot_general(a, b, (dims, ((), ())), preferred_element_type=jnp.float32)


def joined(refs, parts, at):
    return jnp.concatenate([ref[s, :, at] for s in parts for ref in refs], axis=0)


def tiles(width, body):
    step = 256 if width % 256 == 0 else width

    @pl.loop(0, width // step)
    def _(t):
        body(pl.ds(pl.multiple_of(t * step, step), step))


NT, NN = ((1,), (1,)), ((1,), (0,))


def mixes(scores, mix, factors):
    n = scores.shape[1] // 2
    cross = scores[1, :n] - scores[0, n:]
    inmodal = scores[0, :n] - scores[1, n:]
    p_mat = (cross * factors[0:1, 0:1]).astype(jnp.bfloat16)
    q_mat = (inmodal * factors[1:2, 0:1]).astype(jnp.bfloat16)
    mix[0, :n], mix[0, n:] = q_mat, -p_mat
    mix[1, :n], mix[1, n:] = p_mat, -q_mat


def early_kernel(total, n, factors, *refs):
    own, acc, up, down, scores, mix, size = refs[-7:]
    blocks, keys = refs[:n], refs[n:-7]
    scores[...] = jnp.zeros_like(scores)
    size[...] = jnp.zeros_like(size)

    def score(at):
        rows = joined(blocks, (0, 1), at)
        own[:, at] = rows
        for s in range(2):
            scores[s] += dot(rows, joined(keys, (s,), at), NT)
        size[...] += jnp.sum(jnp.abs(rows.astype(jnp.float32)), axis=1, keepdims=True)

    def grad(at):
        acc[:, at] = sum(dot(mix[s], joined(keys, (s,), at), NN) for s in range(2))

    tiles(own.shape[1], score)
    mixes(scores, mix, factors)
    tiles(own.shape[1], grad)
    half = size.shape[0] // 2
    both = size[:half] + size[half:]
    most = both * ((factors[0:1, 0:1] + factors[1:2, 0:1]) * (1.02 * LIMIT * LIMIT * total)) + 1e-30
    up[:half] = TOP / most
    up[half:] = TOP / most
    down[...] = (most / TOP)[: down.shape[0]]


def late_kernel(n, factors, own, acc, up, *refs):
    keys, outs = refs[: -n - 2], refs[-n - 2 : -2]
    scores, mix = refs[-2:]
    rows = outs[0].shape[1]
    scores[...] = jnp.zeros_like(scores)

    def score(at):
        for s in range(2):
            scores[s] += dot(own[:, at], joined(keys, (s,), at), NT)

    def grad(at):
        total = acc[:, at] + sum(dot(mix[s], joined(keys, (s,), at), NN) for s in range(2))
        total = total * up[:, :1]
        for s in range(2):
            for i, out in enumerate(outs):
                out[s, :, at] = total[(s * n + i) * rows : (s * n + i + 1) * rows]

    tiles(own.shape[1], score)
    mixes(scores, mix, factors)
    tiles(own.shape[1], grad)


def call(kernel, operands, out_shape, flops, scratch):
    vmem = pl.BlockSpec(memory_space=pltpu.VMEM)
    moved = sum(x.size * x.dtype.itemsize for x in [*operands, *out_shape])
    return pl.pallas_call(
        kernel,
        out_shape=out_shape,
        in_specs=[vmem] * len(operands),
        out_specs=[vmem] * len(out_shape),
        scratch_shapes=scratch,
        compiler_params=pltpu.CompilerParams(vmem_limit_bytes=40 * 2**20),
        cost_estimate=pl.CostEstimate(flops=flops, bytes_accessed=moved, transcendentals=0),
    )(*operands)


def local(images, texts, loss_weights):
    n_row, n_col = lax.axis_size("row"), lax.axis_size("col")
    row_inner = halves(n_row)[1]
    rows, width = images.shape
    batch = rows * n_row * n_col
    factors = jnp.broadcast_to((loss_weights * (1.0 / math.sqrt(width * batch)))[:, None], (2, 128))
    both = ("row", "col")
    square = [(j, k) for j in range(halves(n_row)[0]) for k in range(halves(n_col)[1])][1:]
    own = jnp.stack([images, texts])

    mine = [own] + [lax.ppermute(own, both, square_shift(n_row, n_col, j, k)) for j, k in square]

    line = [own]
    for which, perm in outer_moves(n_col):
        line.append(lax.ppermute(line[which], "col", perm))

    def pair(block):
        return [lax.ppermute(block, "row", inner_shift(n_row, k)) for k in range(1, row_inner)]

    early, copies = line[:-1], [copy for block in line[:-1] for copy in pair(block)]
    total = rows * len(line) * row_inner
    many = rows * len(mine)
    f32 = jnp.float32

    def flops(keys):
        return 16 * many * width * rows * len(keys)

    def scratch(keys):
        shape = (2, 2 * many, rows * len(keys))
        return [pltpu.VMEM(shape, f32), pltpu.VMEM(shape, images.dtype)]

    mine_joined, acc, up, down = call(
        functools.partial(early_kernel, total, len(mine)),
        [factors] + mine + early,
        [jax.ShapeDtypeStruct((2 * many, width), images.dtype)]
        + [jax.ShapeDtypeStruct(s, f32) for s in [(2 * many, width), (2 * many, 128), (rows, 128)]],
        flops(early),
        scratch(early) + [pltpu.VMEM((2 * many, 128), f32)],
    )
    last, acc = lax.optimization_barrier((line[-1], acc))
    late = copies + [last] + pair(last)
    first, *parts = call(
        functools.partial(late_kernel, len(mine)),
        [factors, mine_joined, acc, up] + late,
        [jax.ShapeDtypeStruct((2, rows, width), f32)] * len(mine),
        flops(late),
        scratch(late),
    )
    back = [
        lax.ppermute(part.astype(jnp.float16), both, square_shift(n_row, n_col, -j, -k))
        for part, (j, k) in zip(parts, square)
    ]
    grads = []
    for s in range(2):
        total = first[s]
        for part in back:
            total = total + part[s].astype(f32)
        grads.append(total * down[:, :1])
    return tuple(grads)


def solution(mesh):
    in_specs = (P(("row", "col"), None), P(("row", "col"), None), P())
    out_specs = (P(("row", "col"), None), P(("row", "col"), None))
    return jax.shard_map(local, mesh=mesh, in_specs=in_specs, out_specs=out_specs, check_vma=False)
```

```python
import functools
import math

import jax
import jax.numpy as jnp
from jax import lax
from jax.experimental import pallas as pl
from jax.experimental.pallas import tpu as pltpu
from jax.sharding import PartitionSpec as P

LIMIT = 6.0
TOP = 32768.0


def halves(count):
    inner = 2 if count % 2 == 0 else 1
    return count // inner, inner


def outer_moves(count):
    outer, inner = halves(count)

    def perm(to):
        return [(i, to(i // inner) * inner + i % inner) for i in range(count)]

    moves = []
    if outer & (outer - 1) == 0:
        held, stride = 1, outer // 2
        while stride:
            moves += [(b, perm(lambda o, s=stride: o ^ s)) for b in range(held)]
            held, stride = 2 * held, stride // 2
    else:
        moves = [(0, perm(lambda o, s=s: (o + s) % outer)) for s in range(1, outer)]
    return moves


def inner_shift(count, step):
    _, inner = halves(count)
    return [(i, i // inner * inner + (i + step) % inner) for i in range(count)]


def square_shift(n_row, n_col, j, k):
    r_outer, r_inner = halves(n_row)
    _, c_inner = halves(n_col)
    pairs = []
    for r in range(n_row):
        for c in range(n_col):
            to_r = (r // r_inner + j) % r_outer * r_inner + r % r_inner
            to_c = c // c_inner * c_inner + (c + k) % c_inner
            pairs.append((r * n_col + c, to_r * n_col + to_c))
    return pairs


def dot(a, b, dims):
    return lax.dot_general(a, b, (dims, ((), ())), preferred_element_type=jnp.float32)


def join(refs):
    return jnp.concatenate([ref[s] for s in range(2) for ref in refs], axis=0)


def weigh(rows, keys, factors):
    n, m = rows.shape[0] // 2, keys.shape[0] // 2
    scores = dot(rows, keys, ((1,), (1,)))
    cross = scores[:n, m:] - scores[n:, :m]
    inmodal = scores[:n, :m] - scores[n:, m:]
    p_mat = (cross * factors[0:1, 0:1]).astype(jnp.bfloat16)
    q_mat = (inmodal * factors[1:2, 0:1]).astype(jnp.bfloat16)
    return p_mat, q_mat


def tiles(width):
    step = 256 if width % 256 == 0 else width
    return [slice(i, i + step) for i in range(0, width, step)]


def tile_grads(p_mat, q_mat, keys, at):
    m = keys.shape[0] // 2
    img, txt = keys[:m, at], keys[m:, at]
    nn = ((1,), (0,))
    grad_img = dot(jnp.concatenate([q_mat, p_mat], axis=1), jnp.concatenate([img, txt]), nn)
    grad_txt = dot(jnp.concatenate([-p_mat, -q_mat], axis=1), jnp.concatenate([img, txt]), nn)
    return grad_img, grad_txt


def bounds(rows, factors, total):
    size = jnp.sum(jnp.abs(rows.astype(jnp.float32)), axis=1, keepdims=True)
    size = size[: size.shape[0] // 2] + size[size.shape[0] // 2 :]
    return size * ((factors[0:1, 0:1] + factors[1:2, 0:1]) * (1.02 * LIMIT * LIMIT * total)) + 1e-30


def early_kernel(total, n, factors, *refs):
    own, acc, up, down = refs[-4:]
    rows = join(refs[:n])
    own[...] = rows
    keys = join(refs[n:-4])
    p_mat, q_mat = weigh(rows, keys, factors)
    for at in tiles(keys.shape[1]):
        acc[0, :, at], acc[1, :, at] = tile_grads(p_mat, q_mat, keys, at)
    most = bounds(rows, factors, total)
    up[...] = jnp.broadcast_to(TOP / most, up.shape)
    down[...] = jnp.broadcast_to((most / TOP)[: down.shape[0]], down.shape)


def late_kernel(total, n, m, factors, own, acc, up, *refs):
    last, early, late, outs = refs[0], refs[1 : m + 1], refs[m + 1 : -n - 1], refs[-n - 1 :]
    rows = last.shape[1]
    keys, every = join(late), join(early + late)
    p_mat, q_mat = weigh(own[...], keys, factors)
    rest = join([last])
    p_rest, q_rest = weigh(rest, every, factors)
    factor = TOP / bounds(rest, factors, total)
    for at in tiles(keys.shape[1]):
        for s, grad in enumerate(tile_grads(p_mat, q_mat, keys, at)):
            grad = (grad + acc[s, :, at]) * up[:, :1]
            for i in range(n):
                outs[i][s, :, at] = grad[i * rows : (i + 1) * rows]
        for s, grad in enumerate(tile_grads(p_rest, q_rest, every, at)):
            outs[n][s, :, at] = grad * factor


def call(kernel, operands, out_shape, flops):
    vmem = pl.BlockSpec(memory_space=pltpu.VMEM)
    moved = sum(x.size * x.dtype.itemsize for x in [*operands, *out_shape])
    return pl.pallas_call(
        kernel,
        out_shape=out_shape,
        in_specs=[vmem] * len(operands),
        out_specs=[vmem] * len(out_shape),
        compiler_params=pltpu.CompilerParams(vmem_limit_bytes=40 * 2**20),
        cost_estimate=pl.CostEstimate(flops=flops, bytes_accessed=moved, transcendentals=0),
    )(*operands)


def local(images, texts, loss_weights):
    n_row, n_col = lax.axis_size("row"), lax.axis_size("col")
    row_inner = halves(n_row)[1]
    rows, width = images.shape
    batch = rows * n_row * n_col
    factors = jnp.broadcast_to((loss_weights * (1.0 / math.sqrt(width * batch)))[:, None], (2, 128))
    both = ("row", "col")
    square = [(j, k) for j in range(halves(n_row)[0]) for k in range(halves(n_col)[1])]
    square = square[2:] + square[1:2]
    own = jnp.stack([images, texts])

    mine = [own] + [lax.ppermute(own, both, square_shift(n_row, n_col, j, k)) for j, k in square]

    line, apart = [own], {0: [images, texts]}
    for step, (which, perm) in enumerate(outer_moves(n_col), 1):
        if which in apart and (which or step == 1):
            apart[step] = [lax.ppermute(half, "col", perm) for half in apart[which]]
            line.append(jnp.stack(apart[step]))
        else:
            line.append(lax.ppermute(line[which], "col", perm))

    def pair(block):
        return [lax.ppermute(block, "row", inner_shift(n_row, k)) for k in range(1, row_inner)]

    early, copies = line[:-1], []
    for block in early:
        if block is own and len(mine) > 1:
            block, mine[1] = lax.optimization_barrier((block, mine[1]))
        copies += pair(block)
    total = rows * len(line) * row_inner
    f32 = jnp.float32
    *first, last = mine
    many = rows * len(first)

    def flops(blocks, keys):
        return 16 * rows * width * rows * blocks * keys

    mine_joined, acc, up, down = call(
        functools.partial(early_kernel, total, len(first)),
        [factors] + first + early,
        [jax.ShapeDtypeStruct((2 * many, width), images.dtype)]
        + [jax.ShapeDtypeStruct(s, f32) for s in [(2, many, width), (many, 128), (rows, 128)]],
        flops(len(first), len(early)),
    )
    late = copies + [line[-1]] + pair(line[-1])
    parts = call(
        functools.partial(late_kernel, total, len(first), len(early)),
        [factors, mine_joined, acc, up, last] + early + late,
        [jax.ShapeDtypeStruct((2, rows, width), f32)] * len(mine),
        flops(len(first), len(late)) + flops(1, len(early + late)),
    )
    far = sorted(zip(square, parts[1:]), key=lambda item: sum(item[0]))
    back = [
        lax.ppermute(part.astype(jnp.float16), both, square_shift(n_row, n_col, -j, -k)) for (j, k), part in far
    ]
    grads = []
    for s in range(2):
        total = parts[0][s]
        for part in back:
            total = total + part[s].astype(f32)
        grads.append(total * down[:, :1])
    return tuple(grads)


def solution(mesh):
    in_specs = (P(("row", "col"), None), P(("row", "col"), None), P())
    out_specs = (P(("row", "col"), None), P(("row", "col"), None))
    return jax.shard_map(local, mesh=mesh, in_specs=in_specs, out_specs=out_specs, check_vma=False)
```

```python
import functools
import math

import jax
import jax.numpy as jnp
from jax import lax
from jax.experimental import pallas as pl
from jax.experimental.pallas import tpu as pltpu
from jax.sharding import PartitionSpec as P

LIMIT = 6.0
TOP = 32768.0


def halves(count):
    inner = 2 if count % 2 == 0 else 1
    return count // inner, inner


def outer_moves(count):
    outer, inner = halves(count)

    def perm(to):
        return [(i, to(i // inner) * inner + i % inner) for i in range(count)]

    moves = []
    if outer & (outer - 1) == 0:
        held, stride = 1, outer // 2
        while stride:
            moves += [(b, perm(lambda o, s=stride: o ^ s)) for b in range(held)]
            held, stride = 2 * held, stride // 2
    else:
        moves = [(0, perm(lambda o, s=s: (o + s) % outer)) for s in range(1, outer)]
    return moves


def inner_shift(count, step):
    _, inner = halves(count)
    return [(i, i // inner * inner + (i + step) % inner) for i in range(count)]


def square_shift(n_row, n_col, j, k):
    r_outer, r_inner = halves(n_row)
    _, c_inner = halves(n_col)
    pairs = []
    for r in range(n_row):
        for c in range(n_col):
            to_r = (r // r_inner + j) % r_outer * r_inner + r % r_inner
            to_c = c // c_inner * c_inner + (c + k) % c_inner
            pairs.append((r * n_col + c, to_r * n_col + to_c))
    return pairs


def dot(a, b, dims):
    return lax.dot_general(a, b, (dims, ((), ())), preferred_element_type=jnp.float32)


def join(refs):
    return jnp.concatenate([ref[s] for s in range(2) for ref in refs], axis=0)


def weigh(rows, keys, factors):
    n, m = rows.shape[0] // 2, keys.shape[0] // 2
    scores = dot(rows, keys, ((1,), (1,)))
    cross = scores[:n, m:] - scores[n:, :m]
    inmodal = scores[:n, :m] - scores[n:, m:]
    p_mat = (cross * factors[0:1, 0:1]).astype(jnp.bfloat16)
    q_mat = (inmodal * factors[1:2, 0:1]).astype(jnp.bfloat16)
    return p_mat, q_mat


def tiles(width):
    step = 256 if width % 256 == 0 else width
    return [slice(i, i + step) for i in range(0, width, step)]


def tile_grads(p_mat, q_mat, keys, at):
    m = keys.shape[0] // 2
    img, txt = keys[:m, at], keys[m:, at]
    nn = ((1,), (0,))
    grad_img = dot(jnp.concatenate([q_mat, p_mat], axis=1), jnp.concatenate([img, txt]), nn)
    grad_txt = dot(jnp.concatenate([-p_mat, -q_mat], axis=1), jnp.concatenate([img, txt]), nn)
    return grad_img, grad_txt


def bounds(rows, factors, total):
    size = jnp.sum(jnp.abs(rows.astype(jnp.float32)), axis=1, keepdims=True)
    size = size[: size.shape[0] // 2] + size[size.shape[0] // 2 :]
    return size * ((factors[0:1, 0:1] + factors[1:2, 0:1]) * (1.02 * LIMIT * LIMIT * total)) + 1e-30


def early_kernel(total, n, factors, *refs):
    own, acc, up, down = refs[-4:]
    rows = join(refs[:n])
    own[...] = rows
    keys = join(refs[n:-4])
    p_mat, q_mat = weigh(rows, keys, factors)
    for at in tiles(keys.shape[1]):
        acc[0, :, at], acc[1, :, at] = tile_grads(p_mat, q_mat, keys, at)
    most = bounds(rows, factors, total)
    up[...] = jnp.broadcast_to(TOP / most, up.shape)
    down[...] = jnp.broadcast_to((most / TOP)[: down.shape[0]], down.shape)


def late_kernel(total, n, m, factors, own, acc, up, *refs):
    last, early, late, outs = refs[0], refs[1 : m + 1], refs[m + 1 : -n - 1], refs[-n - 1 :]
    rows = last.shape[1]
    keys, every = join(late), join(early + late)
    p_mat, q_mat = weigh(own[...], keys, factors)
    rest = join([last])
    p_rest, q_rest = weigh(rest, every, factors)
    factor = TOP / bounds(rest, factors, total)
    for at in tiles(keys.shape[1]):
        for s, grad in enumerate(tile_grads(p_mat, q_mat, keys, at)):
            grad = (grad + acc[s, :, at]) * up[:, :1]
            for i in range(n):
                outs[i][s, :, at] = grad[i * rows : (i + 1) * rows]
        for s, grad in enumerate(tile_grads(p_rest, q_rest, every, at)):
            outs[n][s, :, at] = grad * factor


def call(kernel, operands, out_shape, flops):
    vmem = pl.BlockSpec(memory_space=pltpu.VMEM)
    moved = sum(x.size * x.dtype.itemsize for x in [*operands, *out_shape])
    return pl.pallas_call(
        kernel,
        out_shape=out_shape,
        in_specs=[vmem] * len(operands),
        out_specs=[vmem] * len(out_shape),
        compiler_params=pltpu.CompilerParams(vmem_limit_bytes=40 * 2**20),
        cost_estimate=pl.CostEstimate(flops=flops, bytes_accessed=moved, transcendentals=0),
    )(*operands)


def local(images, texts, loss_weights):
    n_row, n_col = lax.axis_size("row"), lax.axis_size("col")
    row_inner = halves(n_row)[1]
    rows, width = images.shape
    batch = rows * n_row * n_col
    factors = jnp.broadcast_to((loss_weights * (1.0 / math.sqrt(width * batch)))[:, None], (2, 128))
    both = ("row", "col")
    square = [(j, k) for j in range(halves(n_row)[0]) for k in range(halves(n_col)[1])]
    square = square[2:] + square[1:2]
    own = jnp.stack([images, texts])

    mine = [own] + [lax.ppermute(own, both, square_shift(n_row, n_col, j, k)) for j, k in square]

    line, apart = [own], {0: [images, texts]}
    for step, (which, perm) in enumerate(outer_moves(n_col), 1):
        if which in apart and (which or step == 1):
            apart[step] = [lax.ppermute(half, "col", perm) for half in apart[which]]
            line.append(jnp.stack(apart[step]))
        else:
            line.append(lax.ppermute(line[which], "col", perm))

    def pair(block):
        return [lax.ppermute(block, "row", inner_shift(n_row, k)) for k in range(1, row_inner)]

    early, copies = line[:-1], []
    for i, block in enumerate(line[:-1]):
        if i == 0 and len(mine) > 1:
            block, mine[1] = lax.optimization_barrier((block, mine[1]))
        if i == 1 and len(early) > 2:
            block, early[2] = lax.optimization_barrier((block, early[2]))
        copies += pair(block)
    total = rows * len(line) * row_inner
    f32 = jnp.float32
    *first, last = mine
    many = rows * len(first)

    def flops(blocks, keys):
        return 16 * rows * width * rows * blocks * keys

    mine_joined, acc, up, down = call(
        functools.partial(early_kernel, total, len(first)),
        [factors] + first + early,
        [jax.ShapeDtypeStruct((2 * many, width), images.dtype)]
        + [jax.ShapeDtypeStruct(s, f32) for s in [(2, many, width), (many, 128), (rows, 128)]],
        flops(len(first), len(early)),
    )
    late = copies + [line[-1]] + pair(line[-1])
    parts = call(
        functools.partial(late_kernel, total, len(first), len(early)),
        [factors, mine_joined, acc, up, last] + early + late,
        [jax.ShapeDtypeStruct((2, rows, width), f32)] * len(mine),
        flops(len(first), len(late)) + flops(1, len(early + late)),
    )
    far = sorted(zip(square, parts[1:]), key=lambda item: sum(item[0]))
    back = [
        lax.ppermute(part.astype(jnp.float16), both, square_shift(n_row, n_col, -j, -k)) for (j, k), part in far
    ]
    grads = []
    for s in range(2):
        total = parts[0][s]
        for part in back:
            total = total + part[s].astype(f32)
        grads.append(total * down[:, :1])
    return tuple(grads)


def solution(mesh):
    in_specs = (P(("row", "col"), None), P(("row", "col"), None), P())
    out_specs = (P(("row", "col"), None), P(("row", "col"), None))
    return jax.shard_map(local, mesh=mesh, in_specs=in_specs, out_specs=out_specs, check_vma=False)
```

```python
import functools
import math

import jax
import jax.numpy as jnp
from jax import lax
from jax.experimental import pallas as pl
from jax.experimental.pallas import tpu as pltpu
from jax.sharding import PartitionSpec as P

LIMIT = 6.0
TOP = 32768.0


def halves(count):
    inner = 2 if count % 2 == 0 else 1
    return count // inner, inner


def outer_moves(count):
    outer, inner = halves(count)

    def perm(to):
        return [(i, to(i // inner) * inner + i % inner) for i in range(count)]

    moves = []
    if outer & (outer - 1) == 0:
        held, stride = 1, outer // 2
        while stride:
            moves += [(b, perm(lambda o, s=stride: o ^ s)) for b in range(held)]
            held, stride = 2 * held, stride // 2
    else:
        moves = [(0, perm(lambda o, s=s: (o + s) % outer)) for s in range(1, outer)]
    return moves


def inner_shift(count, step):
    _, inner = halves(count)
    return [(i, i // inner * inner + (i + step) % inner) for i in range(count)]


def square_shift(n_row, n_col, j, k):
    r_outer, r_inner = halves(n_row)
    _, c_inner = halves(n_col)
    pairs = []
    for r in range(n_row):
        for c in range(n_col):
            to_r = (r // r_inner + j) % r_outer * r_inner + r % r_inner
            to_c = c // c_inner * c_inner + (c + k) % c_inner
            pairs.append((r * n_col + c, to_r * n_col + to_c))
    return pairs


def dot(a, b, dims):
    return lax.dot_general(a, b, (dims, ((), ())), preferred_element_type=jnp.float32)


def join(refs):
    return jnp.concatenate([ref[s] for s in range(2) for ref in refs], axis=0)


def weigh(rows, keys, factors):
    n, m = rows.shape[0] // 2, keys.shape[0] // 2
    scores = dot(rows, keys, ((1,), (1,)))
    cross = scores[:n, m:] - scores[n:, :m]
    inmodal = scores[:n, :m] - scores[n:, m:]
    p_mat = (cross * factors[0:1, 0:1]).astype(jnp.bfloat16)
    q_mat = (inmodal * factors[1:2, 0:1]).astype(jnp.bfloat16)
    return p_mat, q_mat


def tiles(width):
    step = 256 if width % 256 == 0 else width
    return [slice(i, i + step) for i in range(0, width, step)]


def spread(p_mat, q_mat):
    return jnp.concatenate(
        [jnp.concatenate([q_mat, p_mat], axis=1), jnp.concatenate([-p_mat, -q_mat], axis=1)], axis=0
    )


def bounds(rows, factors, total):
    size = jnp.sum(jnp.abs(rows.astype(jnp.float32)), axis=1, keepdims=True)
    size = size[: size.shape[0] // 2] + size[size.shape[0] // 2 :]
    return size * ((factors[0:1, 0:1] + factors[1:2, 0:1]) * (1.02 * LIMIT * LIMIT * total)) + 1e-30


def early_kernel(total, n, factors, *refs):
    own, acc, up, down = refs[-4:]
    rows = join(refs[:n])
    own[...] = rows
    keys = join(refs[n:-4])
    mix = spread(*weigh(rows, keys, factors))
    for at in tiles(keys.shape[1]):
        acc[:, at] = dot(mix, keys[:, at], ((1,), (0,)))
    most = bounds(rows, factors, total)
    half = most.shape[0]
    for s in range(2):
        up[s * half : (s + 1) * half] = jnp.broadcast_to(TOP / most, (half, up.shape[1]))
    down[...] = jnp.broadcast_to((most / TOP)[: down.shape[0]], down.shape)


def late_kernel(total, n, m, factors, own, acc, up, *refs):
    last, outs = refs[0], refs[-n - 1 :]
    early, late = join(refs[1 : m + 1]), join(refs[m + 1 : -n - 1])
    rows = last.shape[1]
    half = n * rows
    rest = join([last])
    every = jnp.concatenate([own[:half], last[0], own[half:], last[1]], axis=0)
    mix = spread(*weigh(every, late, factors))
    mix_rest = spread(*weigh(rest, early, factors))
    factor = TOP / bounds(rest, factors, total)
    for at in tiles(late.shape[1]):
        grad = dot(mix, late[:, at], ((1,), (0,)))
        grad_rest = dot(mix_rest, early[:, at], ((1,), (0,)))
        for s in range(2):
            low = s * (half + rows)
            mine = slice(s * half, (s + 1) * half)
            ready = (grad[low : low + half] + acc[mine, at]) * up[mine, :1]
            for i in range(n):
                outs[i][s, :, at] = ready[i * rows : (i + 1) * rows]
            both = grad[low + half : low + half + rows] + grad_rest[s * rows : (s + 1) * rows]
            outs[n][s, :, at] = both * factor


def call(kernel, operands, out_shape, flops):
    vmem = pl.BlockSpec(memory_space=pltpu.VMEM)
    moved = sum(x.size * x.dtype.itemsize for x in [*operands, *out_shape])
    return pl.pallas_call(
        kernel,
        out_shape=out_shape,
        in_specs=[vmem] * len(operands),
        out_specs=[vmem] * len(out_shape),
        compiler_params=pltpu.CompilerParams(vmem_limit_bytes=40 * 2**20),
        cost_estimate=pl.CostEstimate(flops=flops, bytes_accessed=moved, transcendentals=0),
    )(*operands)


def local(images, texts, loss_weights):
    n_row, n_col = lax.axis_size("row"), lax.axis_size("col")
    row_inner = halves(n_row)[1]
    rows, width = images.shape
    batch = rows * n_row * n_col
    factors = jnp.broadcast_to((loss_weights * (1.0 / math.sqrt(width * batch)))[:, None], (2, 128))
    both = ("row", "col")
    square = [(j, k) for j in range(halves(n_row)[0]) for k in range(halves(n_col)[1])]
    square = square[2:] + square[1:2]
    own = jnp.stack([images, texts])

    mine = [own] + [lax.ppermute(own, both, square_shift(n_row, n_col, j, k)) for j, k in square]

    line, apart = [own], {0: [images, texts]}
    for step, (which, perm) in enumerate(outer_moves(n_col), 1):
        if which in apart and (which or step == 1):
            apart[step] = [lax.ppermute(half, "col", perm) for half in apart[which]]
            line.append(jnp.stack(apart[step]))
        else:
            line.append(lax.ppermute(line[which], "col", perm))

    def pair(block):
        return [lax.ppermute(block, "row", inner_shift(n_row, k)) for k in range(1, row_inner)]

    early, copies = line[:-1], []
    for i, block in enumerate(line[:-1]):
        if i == 0 and len(mine) > 1:
            block, mine[1] = lax.optimization_barrier((block, mine[1]))
        if i == 1 and len(early) > 2:
            block, early[2] = lax.optimization_barrier((block, early[2]))
        copies += pair(block)
    total = rows * len(line) * row_inner
    f32 = jnp.float32
    *first, last = mine
    many = rows * len(first)

    def flops(blocks, keys):
        return 16 * rows * width * rows * blocks * keys

    mine_joined, acc, up, down = call(
        functools.partial(early_kernel, total, len(first)),
        [factors] + first + early,
        [jax.ShapeDtypeStruct((2 * many, width), images.dtype)]
        + [jax.ShapeDtypeStruct(s, f32) for s in [(2 * many, width), (2 * many, 128), (rows, 128)]],
        flops(len(first), len(early)),
    )
    late = copies + [line[-1]] + pair(line[-1])
    parts = call(
        functools.partial(late_kernel, total, len(first), len(early)),
        [factors, mine_joined, acc, up, last] + early + late,
        [jax.ShapeDtypeStruct((2, rows, width), f32)] * len(mine),
        flops(len(first), len(late)) + flops(1, len(early + late)),
    )
    far = sorted(zip(square, parts[1:]), key=lambda item: sum(item[0]))
    back = [
        lax.ppermute(part.astype(jnp.float16), both, square_shift(n_row, n_col, -j, -k)) for (j, k), part in far
    ]
    ready = [sum((part[s].astype(f32) for part in back[1:]), parts[0][s]) for s in range(2)]
    ready = lax.optimization_barrier(ready)
    grads = [(ready[s] + back[0][s].astype(f32)) * down[:, :1] for s in range(2)]
    return tuple(grads)


def solution(mesh):
    in_specs = (P(("row", "col"), None), P(("row", "col"), None), P())
    out_specs = (P(("row", "col"), None), P(("row", "col"), None))
    return jax.shard_map(local, mesh=mesh, in_specs=in_specs, out_specs=out_specs, check_vma=False)
```

```python
import functools
import math

import jax
import jax.numpy as jnp
from jax import lax
from jax.experimental import pallas as pl
from jax.experimental.pallas import tpu as pltpu
from jax.sharding import PartitionSpec as P

LIMIT = 6.0
TOP = 32768.0


def halves(count):
    inner = 2 if count % 2 == 0 else 1
    return count // inner, inner


def outer_moves(count):
    outer, inner = halves(count)

    def perm(to):
        return [(i, to(i // inner) * inner + i % inner) for i in range(count)]

    moves = []
    if outer & (outer - 1) == 0:
        held, stride = 1, outer // 2
        while stride:
            moves += [(b, perm(lambda o, s=stride: o ^ s)) for b in range(held)]
            held, stride = 2 * held, stride // 2
    else:
        moves = [(0, perm(lambda o, s=s: (o + s) % outer)) for s in range(1, outer)]
    return moves


def inner_shift(count, step):
    _, inner = halves(count)
    return [(i, i // inner * inner + (i + step) % inner) for i in range(count)]


def square_shift(n_row, n_col, j, k):
    r_outer, r_inner = halves(n_row)
    _, c_inner = halves(n_col)
    pairs = []
    for r in range(n_row):
        for c in range(n_col):
            to_r = (r // r_inner + j) % r_outer * r_inner + r % r_inner
            to_c = c // c_inner * c_inner + (c + k) % c_inner
            pairs.append((r * n_col + c, to_r * n_col + to_c))
    return pairs


def dot(a, b, dims):
    return lax.dot_general(a, b, (dims, ((), ())), preferred_element_type=jnp.float32)


def join(refs):
    return jnp.concatenate([ref[s] for s in range(2) for ref in refs], axis=0)


def weigh(rows, keys, factors):
    n, m = rows.shape[0] // 2, keys.shape[0] // 2
    scores = dot(rows, keys, ((1,), (1,)))
    cross = scores[:n, m:] - scores[n:, :m]
    inmodal = scores[:n, :m] - scores[n:, m:]
    p_mat = (cross * factors[0:1, 0:1]).astype(jnp.bfloat16)
    q_mat = (inmodal * factors[1:2, 0:1]).astype(jnp.bfloat16)
    return p_mat, q_mat


def tiles(width):
    step = 256 if width % 256 == 0 else width
    return [slice(i, i + step) for i in range(0, width, step)]


def spread(p_mat, q_mat):
    return jnp.concatenate(
        [jnp.concatenate([q_mat, p_mat], axis=1), jnp.concatenate([-p_mat, -q_mat], axis=1)], axis=0
    )


def bounds(rows, factors, total):
    size = jnp.sum(jnp.abs(rows.astype(jnp.float32)), axis=1, keepdims=True)
    size = size[: size.shape[0] // 2] + size[size.shape[0] // 2 :]
    return size * ((factors[0:1, 0:1] + factors[1:2, 0:1]) * (1.02 * LIMIT * LIMIT * total)) + 1e-30


def early_kernel(total, n, factors, *refs):
    own, acc, up, down = refs[-4:]
    rows = join(refs[:n])
    own[...] = rows
    keys = join(refs[n:-4])
    mix = spread(*weigh(rows, keys, factors))
    for at in tiles(keys.shape[1]):
        acc[:, at] = dot(mix, keys[:, at], ((1,), (0,)))
    most = bounds(rows, factors, total)
    half = most.shape[0]
    for s in range(2):
        up[s * half : (s + 1) * half] = jnp.broadcast_to(TOP / most, (half, up.shape[1]))
    down[...] = jnp.broadcast_to((most / TOP)[: down.shape[0]], down.shape)


def late_kernel(total, n, m, factors, own, acc, up, *refs):
    last, outs = refs[0], refs[-n - 1 :]
    early, late = join(refs[1 : m + 1]), join(refs[m + 1 : -n - 1])
    rows = last.shape[1]
    half = n * rows
    rest = join([last])
    every = jnp.concatenate([own[:half], last[0], own[half:], last[1]], axis=0)
    mix = spread(*weigh(every, late, factors))
    mix_rest = spread(*weigh(rest, early, factors))
    factor = TOP / bounds(rest, factors, total)
    for at in tiles(late.shape[1]):
        grad = dot(mix, late[:, at], ((1,), (0,)))
        grad_rest = dot(mix_rest, early[:, at], ((1,), (0,)))
        for s in range(2):
            low = s * (half + rows)
            mine = slice(s * half, (s + 1) * half)
            ready = (grad[low : low + half] + acc[mine, at]) * up[mine, :1]
            for i in range(n):
                outs[i][s, :, at] = ready[i * rows : (i + 1) * rows]
            both = grad[low + half : low + half + rows] + grad_rest[s * rows : (s + 1) * rows]
            outs[n][s, :, at] = both * factor


def call(kernel, operands, out_shape, flops):
    vmem = pl.BlockSpec(memory_space=pltpu.VMEM)
    moved = sum(x.size * x.dtype.itemsize for x in [*operands, *out_shape])
    return pl.pallas_call(
        kernel,
        out_shape=out_shape,
        in_specs=[vmem] * len(operands),
        out_specs=[vmem] * len(out_shape),
        compiler_params=pltpu.CompilerParams(vmem_limit_bytes=40 * 2**20),
        cost_estimate=pl.CostEstimate(flops=flops, bytes_accessed=moved, transcendentals=0),
    )(*operands)


def local(images, texts, loss_weights):
    n_row, n_col = lax.axis_size("row"), lax.axis_size("col")
    row_inner = halves(n_row)[1]
    rows, width = images.shape
    batch = rows * n_row * n_col
    factors = jnp.broadcast_to((loss_weights * (1.0 / math.sqrt(width * batch)))[:, None], (2, 128))
    both = ("row", "col")
    square = [(j, k) for j in range(halves(n_row)[0]) for k in range(halves(n_col)[1])][1:]
    square.sort(key=lambda place: (sum(map(bool, place)), -place[0]))
    own = jnp.stack([images, texts])

    mine = [own] + [lax.ppermute(own, both, square_shift(n_row, n_col, j, k)) for j, k in square]

    line, apart = [own], {0: [images, texts]}
    for step, (which, perm) in enumerate(outer_moves(n_col), 1):
        if which in apart and (which or step == 1):
            apart[step] = [lax.ppermute(half, "col", perm) for half in apart[which]]
            line.append(jnp.stack(apart[step]))
        else:
            line.append(lax.ppermute(line[which], "col", perm))

    def pair(block):
        return [lax.ppermute(block, "row", inner_shift(n_row, k)) for k in range(1, row_inner)]

    early, copies = line[:-1], []
    for i, block in enumerate(line[:-1]):
        if i < 2 and i + 2 < len(mine):
            block, mine[i + 1] = lax.optimization_barrier((block, mine[i + 1]))
        copies += pair(block)
    total = rows * len(line) * row_inner
    f32 = jnp.float32
    *first, last = mine
    many = rows * len(first)

    def flops(blocks, keys):
        return 16 * rows * width * rows * blocks * keys

    mine_joined, acc, up, down = call(
        functools.partial(early_kernel, total, len(first)),
        [factors] + first + early,
        [jax.ShapeDtypeStruct((2 * many, width), images.dtype)]
        + [jax.ShapeDtypeStruct(s, f32) for s in [(2 * many, width), (2 * many, 128), (rows, 128)]],
        flops(len(first), len(early)),
    )
    late = copies + [line[-1]] + pair(line[-1])
    parts = call(
        functools.partial(late_kernel, total, len(first), len(early)),
        [factors, mine_joined, acc, up, last] + early + late,
        [jax.ShapeDtypeStruct((2, rows, width), f32)] * len(mine),
        flops(len(first), len(late)) + flops(1, len(early + late)),
    )
    far = sorted(zip(square, parts[1:]), key=lambda item: sum(item[0]))
    back = [
        lax.ppermute(part.astype(jnp.float16), both, square_shift(n_row, n_col, -j, -k)) for (j, k), part in far
    ]
    ready = [sum((part[s].astype(f32) for part in back[1:]), parts[0][s]) for s in range(2)]
    ready = lax.optimization_barrier(ready)
    grads = [(ready[s] + back[0][s].astype(f32)) * down[:, :1] for s in range(2)]
    return tuple(grads)


def solution(mesh):
    in_specs = (P(("row", "col"), None), P(("row", "col"), None), P())
    out_specs = (P(("row", "col"), None), P(("row", "col"), None))
    return jax.shard_map(local, mesh=mesh, in_specs=in_specs, out_specs=out_specs, check_vma=False)
```

```python
import functools
import math

import jax
import jax.numpy as jnp
from jax import lax
from jax.experimental import pallas as pl
from jax.experimental.pallas import tpu as pltpu
from jax.sharding import PartitionSpec as P

TOP = 32768.0
LEAST = 2.0**-40


def halves(count):
    inner = 2 if count % 2 == 0 else 1
    return count // inner, inner


def outer_moves(count):
    outer, inner = halves(count)

    def perm(to):
        return [(i, to(i // inner) * inner + i % inner) for i in range(count)]

    moves = []
    if outer & (outer - 1) == 0:
        held, stride = 1, outer // 2
        while stride:
            moves += [(b, perm(lambda o, s=stride: o ^ s)) for b in range(held)]
            held, stride = 2 * held, stride // 2
    else:
        moves = [(0, perm(lambda o, s=s: (o + s) % outer)) for s in range(1, outer)]
    return moves


def inner_shift(count, step):
    _, inner = halves(count)
    return [(i, i // inner * inner + (i + step) % inner) for i in range(count)]


def square_shift(n_row, n_col, j, k):
    r_outer, r_inner = halves(n_row)
    _, c_inner = halves(n_col)
    pairs = []
    for r in range(n_row):
        for c in range(n_col):
            to_r = (r // r_inner + j) % r_outer * r_inner + r % r_inner
            to_c = c // c_inner * c_inner + (c + k) % c_inner
            pairs.append((r * n_col + c, to_r * n_col + to_c))
    return pairs


def dot(a, b, dims):
    return lax.dot_general(a, b, (dims, ((), ())), preferred_element_type=jnp.float32)


def join(refs):
    return jnp.concatenate([ref[s] for s in range(2) for ref in refs], axis=0)


def weigh(rows, keys, factors):
    n, m = rows.shape[0] // 2, keys.shape[0] // 2
    scores = dot(rows, keys, ((1,), (1,)))
    cross = scores[:n, m:] - scores[n:, :m]
    inmodal = scores[:n, :m] - scores[n:, m:]
    p_mat = (cross * factors[0:1, 0:1]).astype(jnp.bfloat16)
    q_mat = (inmodal * factors[1:2, 0:1]).astype(jnp.bfloat16)
    return p_mat, q_mat


def tiles(width):
    step = 256 if width % 256 == 0 else width
    return [slice(i, i + step) for i in range(0, width, step)]


def spread(p_mat, q_mat):
    return jnp.concatenate(
        [jnp.concatenate([q_mat, p_mat], axis=1), jnp.concatenate([-p_mat, -q_mat], axis=1)], axis=0
    )


def bounds(rows, factors, total):
    size = jnp.sum(jnp.abs(rows.astype(jnp.float32)), axis=1, keepdims=True)
    size = size[: size.shape[0] // 2] + size[size.shape[0] // 2 :]
    return size * ((factors[0:1, 0:1] + factors[1:2, 0:1]) * (1.02 * total)) + 1e-25


def largest(keys):
    return jnp.max(jnp.max(jnp.abs(keys.astype(jnp.float32)), axis=0, keepdims=True), axis=1, keepdims=True)


def early_kernel(total, n, factors, *refs):
    own, acc, up, down, most_key = refs[-5:]
    rows = join(refs[:n])
    own[...] = rows
    keys = join(refs[n:-5])
    mix = spread(*weigh(rows, keys, factors))
    for at in tiles(keys.shape[1]):
        acc[:, at] = dot(mix, keys[:, at], ((1,), (0,)))
    most = bounds(rows, factors, total)
    half = most.shape[0]
    for s in range(2):
        up[s * half : (s + 1) * half] = jnp.broadcast_to(TOP / most, (half, up.shape[1]))
    down[...] = jnp.broadcast_to((most / TOP)[: down.shape[0]], down.shape)
    most_key[...] = jnp.broadcast_to(largest(keys), most_key.shape)


def late_kernel(total, n, m, factors, own, acc, up, most_key, *refs):
    last, outs = refs[0], refs[-n - 1 :]
    early, late = join(refs[1 : m + 1]), join(refs[m + 1 : -n - 1])
    rows, width = last.shape[1:]
    half = n * rows
    rest = join([last])
    every = jnp.concatenate([own[:half], last[0], own[half:], last[1]], axis=0)
    mix = spread(*weigh(every, late, factors))
    mix_rest = spread(*weigh(rest, early, factors))
    magnitude = jnp.maximum(jnp.maximum(largest(late), most_key[0:1, 0:1]), LEAST)
    exponent = jnp.ceil(jnp.log2(magnitude))
    shrink = jnp.exp2(-2.0 * exponent)
    factor = TOP / bounds(rest, factors, total)

    def send(out, s, at, values):
        across = width // 128
        for r in range(0, rows, 8):
            for c in range(0, values.shape[1], 128):
                tile = (s * rows + r) // 8 * across + (at.start + c) // 128
                out[tile] = values[r : r + 8, c : c + 128]

    for out in outs[1:]:
        out[out.shape[0] - 1] = jnp.broadcast_to(exponent, (8, 128))
    for at in tiles(width):
        grad = dot(mix, late[:, at], ((1,), (0,)))
        grad_rest = dot(mix_rest, early[:, at], ((1,), (0,)))
        for s in range(2):
            low = s * (half + rows)
            mine = slice(s * half, (s + 1) * half)
            ready = grad[low : low + half] + acc[mine, at]
            outs[0][s, :, at] = ready[:rows]
            ready = ready * up[mine, :1] * shrink
            for i in range(1, n):
                send(outs[i], s, at, ready[i * rows : (i + 1) * rows])
            both = grad[low + half : low + half + rows] + grad_rest[s * rows : (s + 1) * rows]
            send(outs[n], s, at, both * factor * shrink)


def sum_kernel(own, down, *refs):
    *parts, images, texts = refs
    rows, width = images.shape
    across = width // 128
    grow = [jnp.exp2(2.0 * part[part.shape[0] - 1]) for part in parts]
    for s, out in enumerate((images, texts)):
        for r in range(0, rows, 8):
            scales = [down[r : r + 8] * g for g in grow]
            for c in range(across):
                total = own[s, r : r + 8, c * 128 : (c + 1) * 128]
                for part, scale in zip(parts, scales):
                    total = total + part[(s * rows + r) // 8 * across + c] * scale
                out[r : r + 8, c * 128 : (c + 1) * 128] = total


def call(kernel, operands, out_shape, flops):
    vmem = pl.BlockSpec(memory_space=pltpu.VMEM)
    moved = sum(x.size * x.dtype.itemsize for x in [*operands, *out_shape])
    return pl.pallas_call(
        kernel,
        out_shape=out_shape,
        in_specs=[vmem] * len(operands),
        out_specs=[vmem] * len(out_shape),
        compiler_params=pltpu.CompilerParams(vmem_limit_bytes=40 * 2**20),
        cost_estimate=pl.CostEstimate(flops=flops, bytes_accessed=moved, transcendentals=0),
    )(*operands)


def local(images, texts, loss_weights):
    n_row, n_col = lax.axis_size("row"), lax.axis_size("col")
    row_inner = halves(n_row)[1]
    rows, width = images.shape
    batch = rows * n_row * n_col
    factors = jnp.broadcast_to((loss_weights * (1.0 / math.sqrt(width * batch)))[:, None], (2, 128))
    both = ("row", "col")
    square = [(j, k) for j in range(halves(n_row)[0]) for k in range(halves(n_col)[1])]
    square = square[2:] + square[1:2]
    own = jnp.stack([images, texts])

    mine = [own] + [lax.ppermute(own, both, square_shift(n_row, n_col, j, k)) for j, k in square]

    line, apart = [own], {0: [images, texts]}
    for step, (which, perm) in enumerate(outer_moves(n_col), 1):
        if which in apart and (which or step == 1):
            apart[step] = [lax.ppermute(half, "col", perm) for half in apart[which]]
            line.append(jnp.stack(apart[step]))
        else:
            line.append(lax.ppermute(line[which], "col", perm))

    def pair(block):
        return [lax.ppermute(block, "row", inner_shift(n_row, k)) for k in range(1, row_inner)]

    early, copies = line[:-1], []
    for i, block in enumerate(line[:-1]):
        if i == 0 and len(mine) > 1:
            block, mine[1] = lax.optimization_barrier((block, mine[1]))
        if i == 1 and len(early) > 2:
            block, early[2] = lax.optimization_barrier((block, early[2]))
        copies += pair(block)
    total = rows * len(line) * row_inner
    f32 = jnp.float32
    *first, last = mine
    many = rows * len(first)

    def flops(blocks, keys):
        return 16 * rows * width * rows * blocks * keys

    mine_joined, acc, up, down, most_key = call(
        functools.partial(early_kernel, total, len(first)),
        [factors] + first + early,
        [jax.ShapeDtypeStruct((2 * many, width), images.dtype)]
        + [jax.ShapeDtypeStruct(s, f32) for s in [(2 * many, width), (2 * many, 128), (rows, 128), (8, 128)]],
        flops(len(first), len(early)),
    )
    late = copies + [line[-1]] + pair(line[-1])
    parts = call(
        functools.partial(late_kernel, total, len(first), len(early)),
        [factors, mine_joined, acc, up, most_key, last] + early + late,
        [jax.ShapeDtypeStruct((2, rows, width), f32)]
        + [jax.ShapeDtypeStruct((2 * rows * width // 1024 + 1, 8, 128), f32)] * len(square),
        flops(len(first), len(late)) + flops(1, len(early + late)),
    )
    far = sorted(zip(square, parts[1:]), key=lambda item: sum(item[0]))
    back = [
        lax.ppermute(part.astype(jnp.float16), both, square_shift(n_row, n_col, -j, -k)) for (j, k), part in far
    ]
    return tuple(
        call(
            sum_kernel,
            [parts[0], down] + [part.astype(f32) for part in back],
            [jax.ShapeDtypeStruct((rows, width), f32)] * 2,
            4 * rows * width * len(mine),
        )
    )


def solution(mesh):
    in_specs = (P(("row", "col"), None), P(("row", "col"), None), P())
    out_specs = (P(("row", "col"), None), P(("row", "col"), None))
    return jax.shard_map(local, mesh=mesh, in_specs=in_specs, out_specs=out_specs, check_vma=False)
```

```python
import functools
import math

import jax
import jax.numpy as jnp
from jax import lax
from jax.experimental import pallas as pl
from jax.experimental.pallas import tpu as pltpu
from jax.sharding import PartitionSpec as P

TOP = 32768.0
LEAST = 2.0**-40


def halves(count):
    inner = 2 if count % 2 == 0 else 1
    return count // inner, inner


def outer_moves(count):
    outer, inner = halves(count)

    def perm(to):
        return [(i, to(i // inner) * inner + i % inner) for i in range(count)]

    moves = []
    if outer & (outer - 1) == 0:
        held, stride = 1, outer // 2
        while stride:
            moves += [(b, perm(lambda o, s=stride: o ^ s)) for b in range(held)]
            held, stride = 2 * held, stride // 2
    else:
        moves = [(0, perm(lambda o, s=s: (o + s) % outer)) for s in range(1, outer)]
    return moves


def inner_shift(count, step):
    _, inner = halves(count)
    return [(i, i // inner * inner + (i + step) % inner) for i in range(count)]


def square_shift(n_row, n_col, j, k):
    r_outer, r_inner = halves(n_row)
    _, c_inner = halves(n_col)
    pairs = []
    for r in range(n_row):
        for c in range(n_col):
            to_r = (r // r_inner + j) % r_outer * r_inner + r % r_inner
            to_c = c // c_inner * c_inner + (c + k) % c_inner
            pairs.append((r * n_col + c, to_r * n_col + to_c))
    return pairs


def dot(a, b, dims):
    return lax.dot_general(a, b, (dims, ((), ())), preferred_element_type=jnp.float32)


def join(refs):
    return jnp.concatenate([ref[s] for s in range(2) for ref in refs], axis=0)


def weigh(rows, keys, factors):
    n, m = rows.shape[0] // 2, keys.shape[0] // 2
    scores = dot(rows, keys, ((1,), (1,)))
    cross = scores[:n, m:] - scores[n:, :m]
    inmodal = scores[:n, :m] - scores[n:, m:]
    p_mat = (cross * factors[0:1, 0:1]).astype(jnp.bfloat16)
    q_mat = (inmodal * factors[1:2, 0:1]).astype(jnp.bfloat16)
    return p_mat, q_mat


def tiles(width):
    step = 256 if width % 256 == 0 else width
    return [slice(i, i + step) for i in range(0, width, step)]


def spread(p_mat, q_mat):
    return jnp.concatenate(
        [jnp.concatenate([q_mat, p_mat], axis=1), jnp.concatenate([-p_mat, -q_mat], axis=1)], axis=0
    )


def bounds(rows, factors, total):
    size = jnp.sum(jnp.abs(rows.astype(jnp.float32)), axis=1, keepdims=True)
    size = size[: size.shape[0] // 2] + size[size.shape[0] // 2 :]
    return size * ((factors[0:1, 0:1] + factors[1:2, 0:1]) * (1.02 * total)) + 1e-25


def largest(keys):
    return jnp.max(jnp.max(jnp.abs(keys.astype(jnp.float32)), axis=0, keepdims=True), axis=1, keepdims=True)


def early_kernel(total, n, factors, *refs):
    own, acc, up, down, most_key = refs[-5:]
    rows = join(refs[:n])
    own[...] = rows
    keys = join(refs[n:-5])
    mix = spread(*weigh(rows, keys, factors))
    for at in tiles(keys.shape[1]):
        acc[:, at] = dot(mix, keys[:, at], ((1,), (0,)))
    most = bounds(rows, factors, total)
    half = most.shape[0]
    for s in range(2):
        up[s * half : (s + 1) * half] = jnp.broadcast_to(TOP / most, (half, up.shape[1]))
    rows, across = refs[0].shape[1], keys.shape[1] // 128
    for r in range(0, rows, 8):
        tile = jnp.broadcast_to(most[r : r + 8] / TOP, (8, 128))
        for s in range(2):
            for c in range(across):
                down[(s * rows + r) // 8 * across + c] = tile
    most_key[...] = jnp.broadcast_to(largest(keys), most_key.shape)


def late_kernel(total, n, m, factors, own, acc, up, most_key, *refs):
    last, outs = refs[0], refs[-n - 1 :]
    early, late = join(refs[1 : m + 1]), join(refs[m + 1 : -n - 1])
    rows, width = last.shape[1:]
    half = n * rows
    rest = join([last])
    every = jnp.concatenate([own[:half], last[0], own[half:], last[1]], axis=0)
    mix = spread(*weigh(every, late, factors))
    mix_rest = spread(*weigh(rest, early, factors))
    magnitude = jnp.maximum(jnp.maximum(largest(late), most_key[0:1, 0:1]), LEAST)
    exponent = jnp.ceil(jnp.log2(magnitude))
    shrink = jnp.exp2(-2.0 * exponent)
    factor = TOP / bounds(rest, factors, total)

    def send(out, s, at, values):
        across = width // 128
        for r in range(0, rows, 8):
            for c in range(0, values.shape[1], 128):
                tile = (s * rows + r) // 8 * across + (at.start + c) // 128
                out[tile] = values[r : r + 8, c : c + 128]

    for out in outs[1:]:
        out[out.shape[0] - 1] = jnp.broadcast_to(exponent, (8, 128))
    for at in tiles(width):
        grad = dot(mix, late[:, at], ((1,), (0,)))
        grad_rest = dot(mix_rest, early[:, at], ((1,), (0,)))
        for s in range(2):
            low = s * (half + rows)
            mine = slice(s * half, (s + 1) * half)
            ready = grad[low : low + half] + acc[mine, at]
            send(outs[0], s, at, ready[:rows])
            ready = ready * up[mine, :1] * shrink
            for i in range(1, n):
                send(outs[i], s, at, ready[i * rows : (i + 1) * rows])
            both = grad[low + half : low + half + rows] + grad_rest[s * rows : (s + 1) * rows]
            send(outs[n], s, at, both * factor * shrink)


def sum_kernel(ready, down, last, images, texts, total, sems):
    _, rows, width = total.shape
    across = width // 128
    grow = jnp.exp2(2.0 * last[last.shape[0] - 1])
    copies = [pltpu.make_async_copy(total.at[s], out, sems.at[s]) for s, out in enumerate((images, texts))]
    for s, copy in enumerate(copies):
        for r in range(0, rows, 8):
            for c in range(across):
                tile = (s * rows + r) // 8 * across + c
                total[s, r : r + 8, c * 128 : (c + 1) * 128] = ready[tile] + last[tile] * (down[tile] * grow)
        copy.start()
    for copy in copies:
        copy.wait()


def call(kernel, operands, out_shape, flops):
    vmem = pl.BlockSpec(memory_space=pltpu.VMEM)
    moved = sum(x.size * x.dtype.itemsize for x in [*operands, *out_shape])
    return pl.pallas_call(
        kernel,
        out_shape=out_shape,
        in_specs=[vmem] * len(operands),
        out_specs=[vmem] * len(out_shape),
        compiler_params=pltpu.CompilerParams(vmem_limit_bytes=40 * 2**20),
        cost_estimate=pl.CostEstimate(flops=flops, bytes_accessed=moved, transcendentals=0),
    )(*operands)


def local(images, texts, loss_weights):
    n_row, n_col = lax.axis_size("row"), lax.axis_size("col")
    row_inner = halves(n_row)[1]
    rows, width = images.shape
    batch = rows * n_row * n_col
    factors = jnp.broadcast_to((loss_weights * (1.0 / math.sqrt(width * batch)))[:, None], (2, 128))
    both = ("row", "col")
    square = [(j, k) for j in range(halves(n_row)[0]) for k in range(halves(n_col)[1])]
    square = square[2:] + square[1:2]
    own = jnp.stack([images, texts])

    mine = [own] + [lax.ppermute(own, both, square_shift(n_row, n_col, j, k)) for j, k in square]

    line, apart = [own], {0: [images, texts]}
    for step, (which, perm) in enumerate(outer_moves(n_col), 1):
        if which in apart and (which or step == 1):
            apart[step] = [lax.ppermute(half, "col", perm) for half in apart[which]]
            line.append(jnp.stack(apart[step]))
        else:
            line.append(lax.ppermute(line[which], "col", perm))

    def pair(block):
        return [lax.ppermute(block, "row", inner_shift(n_row, k)) for k in range(1, row_inner)]

    early, copies = line[:-1], []
    for i, block in enumerate(line[:-1]):
        if i == 0 and len(mine) > 1:
            block, mine[1] = lax.optimization_barrier((block, mine[1]))
        if i == 1 and len(early) > 2:
            block, early[2] = lax.optimization_barrier((block, early[2]))
        copies += pair(block)
    total = rows * len(line) * row_inner
    f32, count = jnp.float32, 2 * rows * width // 1024
    *first, last = mine
    many = rows * len(first)

    def flops(blocks, keys):
        return 16 * rows * width * rows * blocks * keys

    mine_joined, acc, up, down, most_key = call(
        functools.partial(early_kernel, total, len(first)),
        [factors] + first + early,
        [jax.ShapeDtypeStruct((2 * many, width), images.dtype)]
        + [jax.ShapeDtypeStruct(s, f32) for s in [(2 * many, width), (2 * many, 128), (count, 8, 128), (8, 128)]],
        flops(len(first), len(early)),
    )
    late = copies + [line[-1]] + pair(line[-1])
    parts = call(
        functools.partial(late_kernel, total, len(first), len(early)),
        [factors, mine_joined, acc, up, most_key, last] + early + late,
        [jax.ShapeDtypeStruct((count, 8, 128), f32)]
        + [jax.ShapeDtypeStruct((count + 1, 8, 128), f32)] * len(square),
        flops(len(first), len(late)) + flops(1, len(early + late)),
    )
    far = sorted(zip(square, parts[1:]), key=lambda item: sum(item[0]))
    back = [
        lax.ppermute(part.astype(jnp.float16), both, square_shift(n_row, n_col, -j, -k)) for (j, k), part in far
    ]
    last, *back = [part.astype(f32) for part in back]
    grow = [down * jnp.exp2(2.0 * part[-1, 0, 0]) for part in back]
    ready = parts[0] + sum(part[:-1] * scale for part, scale in zip(back, grow))
    ready = lax.optimization_barrier(ready)
    vmem, hbm = pl.BlockSpec(memory_space=pltpu.VMEM), pl.BlockSpec(memory_space=pltpu.HBM)
    return tuple(
        pl.pallas_call(
            sum_kernel,
            out_shape=[jax.ShapeDtypeStruct((rows, width), f32)] * 2,
            in_specs=[vmem] * 3,
            out_specs=[hbm] * 2,
            scratch_shapes=[pltpu.VMEM((2, rows, width), f32), pltpu.SemaphoreType.DMA((2,))],
            compiler_params=pltpu.CompilerParams(vmem_limit_bytes=40 * 2**20),
        )(ready, down, last)
    )


def solution(mesh):
    in_specs = (P(("row", "col"), None), P(("row", "col"), None), P())
    out_specs = (P(("row", "col"), None), P(("row", "col"), None))
    return jax.shard_map(local, mesh=mesh, in_specs=in_specs, out_specs=out_specs, check_vma=False)
```

```python
import functools
import math

import jax
import jax.numpy as jnp
from jax import lax
from jax.experimental import pallas as pl
from jax.experimental.pallas import tpu as pltpu
from jax.sharding import PartitionSpec as P

TOP = 32768.0
LEAST = 2.0**-40


def halves(count):
    inner = 2 if count % 2 == 0 else 1
    return count // inner, inner


def outer_moves(count):
    outer, inner = halves(count)

    def perm(to):
        return [(i, to(i // inner) * inner + i % inner) for i in range(count)]

    moves = []
    if outer & (outer - 1) == 0:
        held, stride = 1, outer // 2
        while stride:
            moves += [(b, perm(lambda o, s=stride: o ^ s)) for b in range(held)]
            held, stride = 2 * held, stride // 2
    else:
        moves = [(0, perm(lambda o, s=s: (o + s) % outer)) for s in range(1, outer)]
    return moves


def inner_shift(count, step):
    _, inner = halves(count)
    return [(i, i // inner * inner + (i + step) % inner) for i in range(count)]


def square_shift(n_row, n_col, j, k):
    r_outer, r_inner = halves(n_row)
    _, c_inner = halves(n_col)
    pairs = []
    for r in range(n_row):
        for c in range(n_col):
            to_r = (r // r_inner + j) % r_outer * r_inner + r % r_inner
            to_c = c // c_inner * c_inner + (c + k) % c_inner
            pairs.append((r * n_col + c, to_r * n_col + to_c))
    return pairs


def dot(a, b, dims):
    return lax.dot_general(a, b, (dims, ((), ())), preferred_element_type=jnp.float32)


def join(refs):
    return jnp.concatenate([ref[s] for s in range(2) for ref in refs], axis=0)


def weigh(rows, keys, factors):
    n, m = rows.shape[0] // 2, keys.shape[0] // 2
    scores = dot(rows, keys, ((1,), (1,)))
    cross = scores[:n, m:] - scores[n:, :m]
    inmodal = scores[:n, :m] - scores[n:, m:]
    p_mat = (cross * factors[0:1, 0:1]).astype(jnp.bfloat16)
    q_mat = (inmodal * factors[1:2, 0:1]).astype(jnp.bfloat16)
    return p_mat, q_mat


def tiles(width):
    step = 256 if width % 256 == 0 else width
    return [slice(i, i + step) for i in range(0, width, step)]


def spread(p_mat, q_mat):
    return jnp.concatenate(
        [jnp.concatenate([q_mat, p_mat], axis=1), jnp.concatenate([-p_mat, -q_mat], axis=1)], axis=0
    )


def bounds(rows, factors, total):
    size = jnp.sum(jnp.abs(rows.astype(jnp.float32)), axis=1, keepdims=True)
    size = size[: size.shape[0] // 2] + size[size.shape[0] // 2 :]
    return size * ((factors[0:1, 0:1] + factors[1:2, 0:1]) * (1.02 * total)) + 1e-25


def largest(keys):
    return jnp.max(jnp.max(jnp.abs(keys.astype(jnp.float32)), axis=0, keepdims=True), axis=1, keepdims=True)


def early_kernel(total, n, factors, *refs):
    own, acc, up, down, most_key = refs[-5:]
    rows = join(refs[:n])
    own[...] = rows
    keys = join(refs[n:-5])
    mix = spread(*weigh(rows, keys, factors))
    for at in tiles(keys.shape[1]):
        acc[:, at] = dot(mix, keys[:, at], ((1,), (0,)))
    most = bounds(rows, factors, total)
    half = most.shape[0]
    for s in range(2):
        up[s * half : (s + 1) * half] = jnp.broadcast_to(TOP / most, (half, up.shape[1]))
    down[...] = jnp.broadcast_to((most / TOP)[: down.shape[0]], down.shape)
    most_key[...] = jnp.broadcast_to(largest(keys), most_key.shape)


def late_kernel(total, n, m, factors, own, acc, up, most_key, *refs):
    last, outs = refs[0], refs[-n - 1 :]
    early, late = join(refs[1 : m + 1]), join(refs[m + 1 : -n - 1])
    rows, width = last.shape[1:]
    half = n * rows
    rest = join([last])
    every = jnp.concatenate([own[:half], last[0], own[half:], last[1]], axis=0)
    mix = spread(*weigh(every, late, factors))
    mix_rest = spread(*weigh(rest, early, factors))
    magnitude = jnp.maximum(jnp.maximum(largest(late), most_key[0:1, 0:1]), LEAST)
    exponent = jnp.ceil(jnp.log2(magnitude))
    shrink = jnp.exp2(-2.0 * exponent)
    factor = TOP / bounds(rest, factors, total)

    def send(out, s, at, values):
        across = width // 128
        for r in range(0, rows, 8):
            for c in range(0, values.shape[1], 128):
                tile = (s * rows + r) // 8 * across + (at.start + c) // 128
                out[tile] = values[r : r + 8, c : c + 128]

    for out in outs[1:]:
        out[out.shape[0] - 1] = jnp.broadcast_to(exponent, (8, 128))
    for at in tiles(width):
        grad = dot(mix, late[:, at], ((1,), (0,)))
        grad_rest = dot(mix_rest, early[:, at], ((1,), (0,)))
        for s in range(2):
            low = s * (half + rows)
            mine = slice(s * half, (s + 1) * half)
            ready = grad[low : low + half] + acc[mine, at]
            outs[0][s, :, at] = ready[:rows]
            ready = ready * up[mine, :1] * shrink
            for i in range(1, n):
                send(outs[i], s, at, ready[i * rows : (i + 1) * rows])
            both = grad[low + half : low + half + rows] + grad_rest[s * rows : (s + 1) * rows]
            send(outs[n], s, at, both * factor * shrink)


def sum_kernel(own, down, *refs):
    *parts, images, texts = refs
    rows, width = images.shape
    across = width // 128
    grow = [jnp.exp2(2.0 * part[part.shape[0] - 1]) for part in parts]
    for s, out in enumerate((images, texts)):
        for r in range(0, rows, 8):
            scales = [down[r : r + 8] * g for g in grow]
            for c in range(across):
                total = own[s, r : r + 8, c * 128 : (c + 1) * 128]
                for part, scale in zip(parts, scales):
                    total = total + part[(s * rows + r) // 8 * across + c] * scale
                out[r : r + 8, c * 128 : (c + 1) * 128] = total


def call(kernel, operands, out_shape, flops):
    vmem = pl.BlockSpec(memory_space=pltpu.VMEM)
    moved = sum(x.size * x.dtype.itemsize for x in [*operands, *out_shape])
    return pl.pallas_call(
        kernel,
        out_shape=out_shape,
        in_specs=[vmem] * len(operands),
        out_specs=[vmem] * len(out_shape),
        compiler_params=pltpu.CompilerParams(vmem_limit_bytes=40 * 2**20),
        cost_estimate=pl.CostEstimate(flops=flops, bytes_accessed=moved, transcendentals=0),
    )(*operands)


def local(images, texts, loss_weights):
    n_row, n_col = lax.axis_size("row"), lax.axis_size("col")
    row_inner = halves(n_row)[1]
    rows, width = images.shape
    batch = rows * n_row * n_col
    factors = jnp.broadcast_to((loss_weights * (1.0 / math.sqrt(width * batch)))[:, None], (2, 128))
    both = ("row", "col")
    square = [(j, k) for j in range(halves(n_row)[0]) for k in range(halves(n_col)[1])]
    square = square[2:] + square[1:2]
    own = jnp.stack([images, texts])

    mine = [own] + [lax.ppermute(own, both, square_shift(n_row, n_col, j, k)) for j, k in square]

    line, apart = [own], {0: [images, texts]}
    for step, (which, perm) in enumerate(outer_moves(n_col), 1):
        if which in apart and (which or step == 1):
            apart[step] = [lax.ppermute(half, "col", perm) for half in apart[which]]
            line.append(jnp.stack(apart[step]))
        else:
            line.append(lax.ppermute(line[which], "col", perm))

    def pair(block):
        return [lax.ppermute(block, "row", inner_shift(n_row, k)) for k in range(1, row_inner)]

    early, copies = line[:-1], []
    for i, block in enumerate(line[:-1]):
        if i == 0 and len(mine) > 1:
            block, mine[1] = lax.optimization_barrier((block, mine[1]))
        if i == 1 and len(early) > 2:
            block, early[2] = lax.optimization_barrier((block, early[2]))
        copies += pair(block)
    total = rows * len(line) * row_inner
    f32 = jnp.float32
    *first, last = mine
    many = rows * len(first)

    def flops(blocks, keys):
        return 16 * rows * width * rows * blocks * keys

    mine_joined, acc, up, down, most_key = call(
        functools.partial(early_kernel, total, len(first)),
        [factors] + first + early,
        [jax.ShapeDtypeStruct((2 * many, width), images.dtype)]
        + [jax.ShapeDtypeStruct(s, f32) for s in [(2 * many, width), (2 * many, 128), (rows, 128), (8, 128)]],
        flops(len(first), len(early)),
    )
    late = copies + [line[-1]] + pair(line[-1])
    parts = call(
        functools.partial(late_kernel, total, len(first), len(early)),
        [factors, mine_joined, acc, up, most_key, last] + early + late,
        [jax.ShapeDtypeStruct((2, rows, width), f32)]
        + [jax.ShapeDtypeStruct((2 * rows * width // 1024 + 1, 8, 128), f32)] * len(square),
        flops(len(first), len(late)) + flops(1, len(early + late)),
    )
    far = sorted(zip(square, parts[1:]), key=lambda item: (sum(item[0]), item[0][0]))
    back = [
        lax.ppermute(part.astype(jnp.float16), both, square_shift(n_row, n_col, -j, -k)) for (j, k), part in far
    ]
    return tuple(
        call(
            sum_kernel,
            [parts[0], down] + [part.astype(f32) for part in back],
            [jax.ShapeDtypeStruct((rows, width), f32)] * 2,
            4 * rows * width * len(mine),
        )
    )


def solution(mesh):
    in_specs = (P(("row", "col"), None), P(("row", "col"), None), P())
    out_specs = (P(("row", "col"), None), P(("row", "col"), None))
    return jax.shard_map(local, mesh=mesh, in_specs=in_specs, out_specs=out_specs, check_vma=False)
```

```python
import functools
import math

import jax
import jax.numpy as jnp
from jax import lax
from jax.experimental import pallas as pl
from jax.experimental.pallas import tpu as pltpu
from jax.sharding import PartitionSpec as P

TOP = 32768.0
LEAST = 2.0**-40


def halves(count):
    inner = 2 if count % 2 == 0 else 1
    return count // inner, inner


def outer_moves(count):
    outer, inner = halves(count)

    def perm(to):
        return [(i, to(i // inner) * inner + i % inner) for i in range(count)]

    moves = []
    if outer & (outer - 1) == 0:
        held, stride = 1, outer // 2
        while stride:
            moves += [(b, perm(lambda o, s=stride: o ^ s)) for b in range(held)]
            held, stride = 2 * held, stride // 2
    else:
        moves = [(0, perm(lambda o, s=s: (o + s) % outer)) for s in range(1, outer)]
    return moves


def inner_shift(count, step):
    _, inner = halves(count)
    return [(i, i // inner * inner + (i + step) % inner) for i in range(count)]


def square_shift(n_row, n_col, j, k):
    r_outer, r_inner = halves(n_row)
    _, c_inner = halves(n_col)
    pairs = []
    for r in range(n_row):
        for c in range(n_col):
            to_r = (r // r_inner + j) % r_outer * r_inner + r % r_inner
            to_c = c // c_inner * c_inner + (c + k) % c_inner
            pairs.append((r * n_col + c, to_r * n_col + to_c))
    return pairs


def dot(a, b, dims):
    return lax.dot_general(a, b, (dims, ((), ())), preferred_element_type=jnp.float32)


def join(refs):
    return jnp.concatenate([ref[i] for s in range(2) for ref in refs for i in range(s, ref.shape[0], 2)], axis=0)


def weigh(rows, keys, factors):
    n, m = rows.shape[0] // 2, keys.shape[0] // 2
    scores = dot(rows, keys, ((1,), (1,)))
    cross = scores[:n, m:] - scores[n:, :m]
    inmodal = scores[:n, :m] - scores[n:, m:]
    p_mat = (cross * factors[0:1, 0:1]).astype(jnp.bfloat16)
    q_mat = (inmodal * factors[1:2, 0:1]).astype(jnp.bfloat16)
    return p_mat, q_mat


def tiles(width):
    step = 512 if width % 512 == 0 else width
    return [slice(i, i + step) for i in range(0, width, step)]


def spread(p_mat, q_mat):
    return jnp.concatenate(
        [jnp.concatenate([q_mat, p_mat], axis=1), jnp.concatenate([-p_mat, -q_mat], axis=1)], axis=0
    )


def bounds(rows, factors, total):
    size = jnp.sum(jnp.abs(rows.astype(jnp.float32)), axis=1, keepdims=True)
    size = size[: size.shape[0] // 2] + size[size.shape[0] // 2 :]
    return size * ((factors[0:1, 0:1] + factors[1:2, 0:1]) * (1.02 * total)) + 1e-25


def largest(keys):
    return jnp.max(jnp.max(jnp.abs(keys.astype(jnp.float32)), axis=0, keepdims=True), axis=1, keepdims=True)


def early_kernel(total, n, factors, *refs):
    own, acc, up, down, most_key = refs[-5:]
    rows = join(refs[:n])
    own[...] = rows
    keys = join(refs[n:-5])
    mix = spread(*weigh(rows, keys, factors))
    for at in tiles(keys.shape[1]):
        acc[:, at] = dot(mix, keys[:, at], ((1,), (0,)))
    most = bounds(rows, factors, total)
    half = most.shape[0]
    for s in range(2):
        up[s * half : (s + 1) * half] = jnp.broadcast_to(TOP / most, (half, up.shape[1]))
    down[...] = jnp.broadcast_to((most / TOP)[: down.shape[0]], down.shape)
    most_key[...] = jnp.broadcast_to(largest(keys), most_key.shape)


def late_kernel(total, n, m, factors, own, acc, up, most_key, *refs):
    last, outs = refs[0], refs[-n - 1 :]
    early, late = join(refs[1 : m + 1]), join(refs[m + 1 : -n - 1])
    rows, width = last.shape[1:]
    half = n * rows
    rest = join([last])
    every = jnp.concatenate([own[:half], last[0], own[half:], last[1]], axis=0)
    mix = spread(*weigh(every, late, factors))
    mix_rest = spread(*weigh(rest, early, factors))
    magnitude = jnp.maximum(jnp.maximum(largest(late), most_key[0:1, 0:1]), LEAST)
    exponent = jnp.ceil(jnp.log2(magnitude))
    shrink = jnp.exp2(-2.0 * exponent)
    factor = TOP / bounds(rest, factors, total)

    def send(out, s, at, values):
        across = width // 128
        for r in range(0, rows, 8):
            for c in range(0, values.shape[1], 128):
                tile = (s * rows + r) // 8 * across + (at.start + c) // 128
                out[tile] = values[r : r + 8, c : c + 128]

    for out in outs[1:]:
        out[out.shape[0] - 1] = jnp.broadcast_to(exponent, (8, 128))
    for at in tiles(width):
        grad = dot(mix, late[:, at], ((1,), (0,)))
        grad_rest = dot(mix_rest, early[:, at], ((1,), (0,)))
        for s in range(2):
            low = s * (half + rows)
            mine = slice(s * half, (s + 1) * half)
            ready = grad[low : low + half] + acc[mine, at]
            outs[0][s, :, at] = ready[:rows]
            ready = ready * up[mine, :1] * shrink
            for i in range(1, n):
                send(outs[i], s, at, ready[i * rows : (i + 1) * rows])
            both = grad[low + half : low + half + rows] + grad_rest[s * rows : (s + 1) * rows]
            send(outs[n], s, at, both * factor * shrink)


def sum_kernel(own, down, *refs):
    *parts, images, texts = refs
    rows, width = images.shape
    across = width // 128
    grow = [jnp.exp2(2.0 * part[part.shape[0] - 1]) for part in parts]
    for s, out in enumerate((images, texts)):
        for r in range(0, rows, 8):
            scales = [down[r : r + 8] * g for g in grow]
            for c in range(across):
                total = own[s, r : r + 8, c * 128 : (c + 1) * 128]
                for part, scale in zip(parts, scales):
                    total = total + part[(s * rows + r) // 8 * across + c] * scale
                out[r : r + 8, c * 128 : (c + 1) * 128] = total


def call(kernel, operands, out_shape, flops):
    vmem = pl.BlockSpec(memory_space=pltpu.VMEM)
    moved = sum(x.size * x.dtype.itemsize for x in [*operands, *out_shape])
    return pl.pallas_call(
        kernel,
        out_shape=out_shape,
        in_specs=[vmem] * len(operands),
        out_specs=[vmem] * len(out_shape),
        compiler_params=pltpu.CompilerParams(vmem_limit_bytes=40 * 2**20),
        cost_estimate=pl.CostEstimate(flops=flops, bytes_accessed=moved, transcendentals=0),
    )(*operands)


def local(images, texts, loss_weights):
    n_row, n_col = lax.axis_size("row"), lax.axis_size("col")
    row_inner = halves(n_row)[1]
    rows, width = images.shape
    batch = rows * n_row * n_col
    factors = jnp.broadcast_to((loss_weights * (1.0 / math.sqrt(width * batch)))[:, None], (2, 128))
    both = ("row", "col")
    square = [(j, k) for j in range(halves(n_row)[0]) for k in range(halves(n_col)[1])]
    square = square[2:] + square[1:2]
    own = jnp.stack([images, texts])

    mine = [own] + [lax.ppermute(own, both, square_shift(n_row, n_col, j, k)) for j, k in square]

    line, apart = [own], {0: [images, texts]}
    for step, (which, perm) in enumerate(outer_moves(n_col), 1):
        if which in apart and (which or step == 1):
            apart[step] = [lax.ppermute(half, "col", perm) for half in apart[which]]
            line.append(jnp.stack(apart[step]))
        else:
            line.append(lax.ppermute(line[which], "col", perm))

    def pair(block):
        return [lax.ppermute(block, "row", inner_shift(n_row, k)) for k in range(1, row_inner)]

    early, copies = line[:-1], []
    for i, block in enumerate(line[:-1]):
        if i == 0 and len(mine) > 1:
            block, mine[1] = lax.optimization_barrier((block, mine[1]))
        if i == 1 and len(early) > 2:
            block, early[2] = lax.optimization_barrier((block, early[2]))
        copies += pair(block)
    total = rows * len(line) * row_inner
    f32 = jnp.float32
    *first, last = mine
    many = rows * len(first)

    def flops(blocks, keys):
        return 16 * rows * width * rows * blocks * keys

    mine_joined, acc, up, down, most_key = call(
        functools.partial(early_kernel, total, len(first)),
        [factors] + first + early,
        [jax.ShapeDtypeStruct((2 * many, width), images.dtype)]
        + [jax.ShapeDtypeStruct(s, f32) for s in [(2 * many, width), (2 * many, 128), (rows, 128), (8, 128)]],
        flops(len(first), len(early)),
    )
    late = copies + [line[-1]] + pair(line[-1])
    parts = call(
        functools.partial(late_kernel, total, len(first), len(early)),
        [factors, mine_joined, acc, up, most_key, last] + early + late,
        [jax.ShapeDtypeStruct((2, rows, width), f32)]
        + [jax.ShapeDtypeStruct((2 * rows * width // 1024 + 1, 8, 128), f32)] * len(square),
        flops(len(first), len(late)) + flops(1, len(early + late)),
    )
    far = sorted(zip(square, parts[1:]), key=lambda item: sum(item[0]))
    back = [
        lax.ppermute(part.astype(jnp.float16), both, square_shift(n_row, n_col, -j, -k)) for (j, k), part in far
    ]
    return tuple(
        call(
            sum_kernel,
            [parts[0], down] + [part.astype(f32) for part in back],
            [jax.ShapeDtypeStruct((rows, width), f32)] * 2,
            4 * rows * width * len(mine),
        )
    )


def solution(mesh):
    in_specs = (P(("row", "col"), None), P(("row", "col"), None), P())
    out_specs = (P(("row", "col"), None), P(("row", "col"), None))
    return jax.shard_map(local, mesh=mesh, in_specs=in_specs, out_specs=out_specs, check_vma=False)
```

```python
import functools
import math

import jax
import jax.numpy as jnp
from jax import lax
from jax.experimental import pallas as pl
from jax.experimental.pallas import tpu as pltpu
from jax.sharding import PartitionSpec as P

TOP = 32768.0
LEAST = 2.0**-40


def halves(count):
    inner = 2 if count % 2 == 0 else 1
    return count // inner, inner


def outer_moves(count):
    outer, inner = halves(count)

    def perm(to):
        return [(i, to(i // inner) * inner + i % inner) for i in range(count)]

    moves = []
    if outer & (outer - 1) == 0:
        held, stride = 1, outer // 2
        while stride:
            moves += [(b, perm(lambda o, s=stride: o ^ s)) for b in range(held)]
            held, stride = 2 * held, stride // 2
    else:
        moves = [(0, perm(lambda o, s=s: (o + s) % outer)) for s in range(1, outer)]
    return moves


def inner_shift(count, step):
    _, inner = halves(count)
    return [(i, i // inner * inner + (i + step) % inner) for i in range(count)]


def square_shift(n_row, n_col, j, k):
    r_outer, r_inner = halves(n_row)
    _, c_inner = halves(n_col)
    pairs = []
    for r in range(n_row):
        for c in range(n_col):
            to_r = (r // r_inner + j) % r_outer * r_inner + r % r_inner
            to_c = c // c_inner * c_inner + (c + k) % c_inner
            pairs.append((r * n_col + c, to_r * n_col + to_c))
    return pairs


def dot(a, b, dims):
    return lax.dot_general(a, b, (dims, ((), ())), preferred_element_type=jnp.float32)


def join(refs):
    return jnp.concatenate([ref[s] for s in range(2) for ref in refs], axis=0)


def weigh(rows, keys, factors):
    n, m = rows.shape[0] // 2, keys.shape[0] // 2
    scores = dot(rows, keys, ((1,), (1,)))
    cross = scores[:n, m:] - scores[n:, :m]
    inmodal = scores[:n, :m] - scores[n:, m:]
    p_mat = (cross * factors[0:1, 0:1]).astype(jnp.bfloat16)
    q_mat = (inmodal * factors[1:2, 0:1]).astype(jnp.bfloat16)
    return p_mat, q_mat


def tiles(width):
    step = 256 if width % 256 == 0 else width
    return [slice(i, i + step) for i in range(0, width, step)]


def spread(p_mat, q_mat):
    return jnp.concatenate(
        [jnp.concatenate([q_mat, p_mat], axis=1), jnp.concatenate([-p_mat, -q_mat], axis=1)], axis=0
    )


def bounds(rows, factors, total):
    size = jnp.sum(jnp.abs(rows.astype(jnp.float32)), axis=1, keepdims=True)
    size = size[: size.shape[0] // 2] + size[size.shape[0] // 2 :]
    return size * ((factors[0:1, 0:1] + factors[1:2, 0:1]) * (1.02 * total)) + 1e-25


def largest(keys):
    return jnp.max(jnp.max(jnp.abs(keys.astype(jnp.float32)), axis=0, keepdims=True), axis=1, keepdims=True)


def early_kernel(total, n, factors, *refs):
    own, acc, up, down, most_key = refs[-5:]
    rows = join(refs[:n])
    own[...] = rows
    keys = join(refs[n:-5])
    mix = spread(*weigh(rows, keys, factors))
    for at in tiles(keys.shape[1]):
        acc[:, at] = dot(mix, keys[:, at], ((1,), (0,)))
    most = bounds(rows, factors, total)
    half = most.shape[0]
    for s in range(2):
        up[s * half : (s + 1) * half] = jnp.broadcast_to(TOP / most, (half, up.shape[1]))
    down[...] = jnp.broadcast_to((most / TOP)[: down.shape[0]], down.shape)
    most_key[...] = jnp.broadcast_to(largest(keys), most_key.shape)


def late_kernel(total, n, m, factors, own, acc, up, most_key, *refs):
    last, outs = refs[0], refs[-n - 1 :]
    early, late = join(refs[1 : m + 1]), join(refs[m + 1 : -n - 1])
    rows, width = last.shape[1:]
    half = n * rows
    rest = join([last])
    every = jnp.concatenate([own[:half], last[0], own[half:], last[1]], axis=0)
    mix = spread(*weigh(every, late, factors))
    mix_rest = spread(*weigh(rest, early, factors))
    magnitude = jnp.maximum(jnp.maximum(largest(late), most_key[0:1, 0:1]), LEAST)
    exponent = jnp.ceil(jnp.log2(magnitude))
    shrink = jnp.exp2(-2.0 * exponent)
    factor = TOP / bounds(rest, factors, total)

    def send(out, s, at, values):
        across = width // 128
        for r in range(0, rows, 8):
            for c in range(0, values.shape[1], 128):
                tile = (s * rows + r) // 8 * across + (at.start + c) // 128
                out[tile] = values[r : r + 8, c : c + 128]

    for out in outs[1:]:
        out[out.shape[0] - 1] = jnp.broadcast_to(exponent, (8, 128))
    for at in tiles(width):
        grad = dot(mix, late[:, at], ((1,), (0,)))
        grad_rest = dot(mix_rest, early[:, at], ((1,), (0,)))
        for s in range(2):
            low = s * (half + rows)
            mine = slice(s * half, (s + 1) * half)
            ready = grad[low : low + half] + acc[mine, at]
            outs[0][s, :, at] = ready[:rows]
            ready = ready * up[mine, :1] * shrink
            for i in range(1, n):
                send(outs[i], s, at, ready[i * rows : (i + 1) * rows])
            both = grad[low + half : low + half + rows] + grad_rest[s * rows : (s + 1) * rows]
            send(outs[n], s, at, both * factor * shrink)


def sum_kernel(own, down, *refs):
    *parts, images, texts = refs
    rows, width = images.shape
    across = width // 128
    grow = [jnp.exp2(2.0 * part[part.shape[0] - 1]) for part in parts]
    for s, out in enumerate((images, texts)):
        for r in range(0, rows, 8):
            scales = [down[r : r + 8] * g for g in grow]
            for c in range(across):
                total = own[s, r : r + 8, c * 128 : (c + 1) * 128]
                for part, scale in zip(parts, scales):
                    total = total + part[(s * rows + r) // 8 * across + c] * scale
                out[r : r + 8, c * 128 : (c + 1) * 128] = total


def call(kernel, operands, out_shape, flops):
    vmem = pl.BlockSpec(memory_space=pltpu.VMEM)
    moved = sum(x.size * x.dtype.itemsize for x in [*operands, *out_shape])
    return pl.pallas_call(
        kernel,
        out_shape=out_shape,
        in_specs=[vmem] * len(operands),
        out_specs=[vmem] * len(out_shape),
        compiler_params=pltpu.CompilerParams(vmem_limit_bytes=40 * 2**20),
        cost_estimate=pl.CostEstimate(flops=flops, bytes_accessed=moved, transcendentals=0),
    )(*operands)


def local(images, texts, loss_weights):
    n_row, n_col = lax.axis_size("row"), lax.axis_size("col")
    row_inner = halves(n_row)[1]
    rows, width = images.shape
    batch = rows * n_row * n_col
    factors = jnp.broadcast_to((loss_weights * (1.0 / math.sqrt(width * batch)))[:, None], (2, 128))
    both = ("row", "col")
    square = [(j, k) for j in range(halves(n_row)[0]) for k in range(halves(n_col)[1])]
    square = square[1:2] + square[3:] + square[2:3]
    own = jnp.stack([images, texts])

    mine = [own] + [lax.ppermute(own, both, square_shift(n_row, n_col, j, k)) for j, k in square]

    line, apart = [own], {0: [images, texts]}
    for step, (which, perm) in enumerate(outer_moves(n_col), 1):
        if which in apart and (which or step == 1):
            apart[step] = [lax.ppermute(half, "col", perm) for half in apart[which]]
            line.append(jnp.stack(apart[step]))
        else:
            line.append(lax.ppermute(line[which], "col", perm))

    def pair(block):
        return [lax.ppermute(block, "row", inner_shift(n_row, k)) for k in range(1, row_inner)]

    early, copies = line[:-1], []
    for i, block in enumerate(line[:-1]):
        if i == 0 and len(mine) > 1:
            block, mine[1] = lax.optimization_barrier((block, mine[1]))
        if i == 1 and len(early) > 2:
            block, early[2] = lax.optimization_barrier((block, early[2]))
        copies += pair(block)
    total = rows * len(line) * row_inner
    f32 = jnp.float32
    *first, last = mine
    many = rows * len(first)

    def flops(blocks, keys):
        return 16 * rows * width * rows * blocks * keys

    mine_joined, acc, up, down, most_key = call(
        functools.partial(early_kernel, total, len(first)),
        [factors] + first + early,
        [jax.ShapeDtypeStruct((2 * many, width), images.dtype)]
        + [jax.ShapeDtypeStruct(s, f32) for s in [(2 * many, width), (2 * many, 128), (rows, 128), (8, 128)]],
        flops(len(first), len(early)),
    )
    late = copies + [line[-1]] + pair(line[-1])
    parts = call(
        functools.partial(late_kernel, total, len(first), len(early)),
        [factors, mine_joined, acc, up, most_key, last] + early + late,
        [jax.ShapeDtypeStruct((2, rows, width), f32)]
        + [jax.ShapeDtypeStruct((2 * rows * width // 1024 + 1, 8, 128), f32)] * len(square),
        flops(len(first), len(late)) + flops(1, len(early + late)),
    )
    far = sorted(zip(square, parts[1:]), key=lambda item: sum(item[0]))
    back = [
        lax.ppermute(part.astype(jnp.float16), both, square_shift(n_row, n_col, -j, -k)) for (j, k), part in far
    ]
    return tuple(
        call(
            sum_kernel,
            [parts[0], down] + [part.astype(f32) for part in back],
            [jax.ShapeDtypeStruct((rows, width), f32)] * 2,
            4 * rows * width * len(mine),
        )
    )


def solution(mesh):
    in_specs = (P(("row", "col"), None), P(("row", "col"), None), P())
    out_specs = (P(("row", "col"), None), P(("row", "col"), None))
    return jax.shard_map(local, mesh=mesh, in_specs=in_specs, out_specs=out_specs, check_vma=False)
```

```python
import functools
import math

import jax
import jax.numpy as jnp
from jax import lax
from jax.experimental import pallas as pl
from jax.experimental.pallas import tpu as pltpu
from jax.sharding import PartitionSpec as P

TOP = 32768.0
LEAST = 2.0**-40


def halves(count):
    inner = 2 if count % 2 == 0 else 1
    return count // inner, inner


def outer_moves(count):
    outer, inner = halves(count)

    def perm(to):
        return [(i, to(i // inner) * inner + i % inner) for i in range(count)]

    moves = []
    if outer & (outer - 1) == 0:
        held, stride = 1, outer // 2
        while stride:
            moves += [(b, perm(lambda o, s=stride: o ^ s)) for b in range(held)]
            held, stride = 2 * held, stride // 2
    else:
        moves = [(0, perm(lambda o, s=s: (o + s) % outer)) for s in range(1, outer)]
    return moves


def inner_shift(count, step):
    _, inner = halves(count)
    return [(i, i // inner * inner + (i + step) % inner) for i in range(count)]


def square_shift(n_row, n_col, j, k):
    r_outer, r_inner = halves(n_row)
    _, c_inner = halves(n_col)
    pairs = []
    for r in range(n_row):
        for c in range(n_col):
            to_r = (r // r_inner + j) % r_outer * r_inner + r % r_inner
            to_c = c // c_inner * c_inner + (c + k) % c_inner
            pairs.append((r * n_col + c, to_r * n_col + to_c))
    return pairs


def dot(a, b, dims):
    return lax.dot_general(a, b, (dims, ((), ())), preferred_element_type=jnp.float32)


def join(refs):
    return jnp.concatenate([ref[s] for s in range(2) for ref in refs], axis=0)


def weigh(rows, keys, factors):
    n, m = rows.shape[0] // 2, keys.shape[0] // 2
    scores = dot(rows, keys, ((1,), (1,)))
    cross = scores[:n, m:] - scores[n:, :m]
    inmodal = scores[:n, :m] - scores[n:, m:]
    p_mat = (cross * factors[0:1, 0:1]).astype(jnp.bfloat16)
    q_mat = (inmodal * factors[1:2, 0:1]).astype(jnp.bfloat16)
    return p_mat, q_mat


def tiles(width):
    step = 256 if width % 256 == 0 else width
    return [slice(i, i + step) for i in range(0, width, step)]


def spread(p_mat, q_mat):
    return jnp.concatenate(
        [jnp.concatenate([q_mat, p_mat], axis=1), jnp.concatenate([-p_mat, -q_mat], axis=1)], axis=0
    )


def bounds(rows, factors, total):
    size = jnp.sum(jnp.abs(rows.astype(jnp.float32)), axis=1, keepdims=True)
    size = size[: size.shape[0] // 2] + size[size.shape[0] // 2 :]
    return size * ((factors[0:1, 0:1] + factors[1:2, 0:1]) * (1.02 * total)) + 1e-25


def largest(keys):
    return jnp.max(jnp.max(jnp.abs(keys.astype(jnp.float32)), axis=0, keepdims=True), axis=1, keepdims=True)


def early_kernel(total, n, factors, *refs):
    own, acc, up, down, most_key = refs[-5:]
    rows = join(refs[:n])
    own[...] = rows
    keys = join(refs[n:-5])
    mix = spread(*weigh(rows, keys, factors))
    for at in tiles(keys.shape[1]):
        acc[:, at] = dot(mix, keys[:, at], ((1,), (0,)))
    most = bounds(rows, factors, total)
    half = most.shape[0]
    for s in range(2):
        up[s * half : (s + 1) * half] = jnp.broadcast_to(TOP / most, (half, up.shape[1]))
    down[...] = jnp.broadcast_to((most / TOP)[: down.shape[0]], down.shape)
    most_key[...] = jnp.broadcast_to(largest(keys), most_key.shape)


def late_kernel(total, n, m, factors, own, acc, up, most_key, *refs):
    last, outs = refs[0], refs[-n - 1 :]
    early, late = join(refs[1 : m + 1]), join(refs[m + 1 : -n - 1])
    rows, width = last.shape[1:]
    half = n * rows
    rest = join([last])
    every = jnp.concatenate([own[:half], last[0], own[half:], last[1]], axis=0)
    mix = spread(*weigh(every, late, factors))
    mix_rest = spread(*weigh(rest, early, factors))
    magnitude = jnp.maximum(jnp.maximum(largest(late), most_key[0:1, 0:1]), LEAST)
    exponent = jnp.ceil(jnp.log2(magnitude))
    shrink = jnp.exp2(-2.0 * exponent)
    factor = TOP / bounds(rest, factors, total)

    def send(out, s, at, values):
        across = width // 128
        for r in range(0, rows, 8):
            for c in range(0, values.shape[1], 128):
                tile = (s * rows + r) // 8 * across + (at.start + c) // 128
                out[tile] = values[r : r + 8, c : c + 128]

    for out in outs[1:]:
        out[out.shape[0] - 1] = jnp.broadcast_to(exponent, (8, 128))
    for at in tiles(width):
        grad = dot(mix, late[:, at], ((1,), (0,)))
        grad_rest = dot(mix_rest, early[:, at], ((1,), (0,)))
        for s in range(2):
            low = s * (half + rows)
            mine = slice(s * half, (s + 1) * half)
            ready = grad[low : low + half] + acc[mine, at]
            outs[0][s, :, at] = ready[:rows]
            ready = ready * up[mine, :1] * shrink
            for i in range(1, n):
                send(outs[i], s, at, ready[i * rows : (i + 1) * rows])
            both = grad[low + half : low + half + rows] + grad_rest[s * rows : (s + 1) * rows]
            send(outs[n], s, at, both * factor * shrink)


def sum_kernel(own, down, *refs):
    *parts, images, texts = refs
    rows, width = images.shape
    across = width // 128
    grow = [jnp.exp2(2.0 * part[part.shape[0] - 1]) for part in parts]
    for s, out in enumerate((images, texts)):
        for r in range(0, rows, 8):
            scales = [down[r : r + 8] * g for g in grow]
            for c in range(across):
                total = own[s, r : r + 8, c * 128 : (c + 1) * 128]
                for part, scale in zip(parts, scales):
                    total = total + part[(s * rows + r) // 8 * across + c] * scale
                out[r : r + 8, c * 128 : (c + 1) * 128] = total


def call(kernel, operands, out_shape, flops):
    vmem = pl.BlockSpec(memory_space=pltpu.VMEM)
    moved = sum(x.size * x.dtype.itemsize for x in [*operands, *out_shape])
    return pl.pallas_call(
        kernel,
        out_shape=out_shape,
        in_specs=[vmem] * len(operands),
        out_specs=[vmem] * len(out_shape),
        compiler_params=pltpu.CompilerParams(vmem_limit_bytes=40 * 2**20),
        cost_estimate=pl.CostEstimate(flops=flops, bytes_accessed=moved, transcendentals=0),
    )(*operands)


def local(images, texts, loss_weights):
    n_row, n_col = lax.axis_size("row"), lax.axis_size("col")
    row_inner = halves(n_row)[1]
    rows, width = images.shape
    batch = rows * n_row * n_col
    factors = jnp.broadcast_to((loss_weights * (1.0 / math.sqrt(width * batch)))[:, None], (2, 128))
    both = ("row", "col")
    square = [(j, k) for j in range(halves(n_row)[0]) for k in range(halves(n_col)[1])]
    square = sorted(square[1:], key=lambda place: (all(place), not place[0]))
    own = jnp.stack([images, texts])

    mine = [own] + [lax.ppermute(own, both, square_shift(n_row, n_col, j, k)) for j, k in square]

    line, apart = [own], {0: [images, texts]}
    for step, (which, perm) in enumerate(outer_moves(n_col), 1):
        if which in apart and (which or step == 1):
            apart[step] = [lax.ppermute(half, "col", perm) for half in apart[which]]
            line.append(jnp.stack(apart[step]))
        else:
            line.append(lax.ppermute(line[which], "col", perm))

    def pair(block):
        return [lax.ppermute(block, "row", inner_shift(n_row, k)) for k in range(1, row_inner)]

    early, copies = line[:-1], []
    for i, block in enumerate(line[:-1]):
        if i == 0 and len(mine) > 1:
            block, mine[1] = lax.optimization_barrier((block, mine[1]))
        copies += pair(block)
    total = rows * len(line) * row_inner
    f32 = jnp.float32
    *first, last = mine
    many = rows * len(first)

    def flops(blocks, keys):
        return 16 * rows * width * rows * blocks * keys

    mine_joined, acc, up, down, most_key = call(
        functools.partial(early_kernel, total, len(first)),
        [factors] + first + early,
        [jax.ShapeDtypeStruct((2 * many, width), images.dtype)]
        + [jax.ShapeDtypeStruct(s, f32) for s in [(2 * many, width), (2 * many, 128), (rows, 128), (8, 128)]],
        flops(len(first), len(early)),
    )
    late = copies + [line[-1]] + pair(line[-1])
    parts = call(
        functools.partial(late_kernel, total, len(first), len(early)),
        [factors, mine_joined, acc, up, most_key, last] + early + late,
        [jax.ShapeDtypeStruct((2, rows, width), f32)]
        + [jax.ShapeDtypeStruct((2 * rows * width // 1024 + 1, 8, 128), f32)] * len(square),
        flops(len(first), len(late)) + flops(1, len(early + late)),
    )
    far = sorted(zip(square, parts[1:]), key=lambda item: sum(item[0]))
    back = [
        lax.ppermute(part.astype(jnp.float16), both, square_shift(n_row, n_col, -j, -k)) for (j, k), part in far
    ]
    return tuple(
        call(
            sum_kernel,
            [parts[0], down] + [part.astype(f32) for part in back],
            [jax.ShapeDtypeStruct((rows, width), f32)] * 2,
            4 * rows * width * len(mine),
        )
    )


def solution(mesh):
    in_specs = (P(("row", "col"), None), P(("row", "col"), None), P())
    out_specs = (P(("row", "col"), None), P(("row", "col"), None))
    return jax.shard_map(local, mesh=mesh, in_specs=in_specs, out_specs=out_specs, check_vma=False)
```

```python
import functools
import math

import jax
import jax.numpy as jnp
from jax import lax
from jax.experimental import pallas as pl
from jax.experimental.pallas import tpu as pltpu
from jax.sharding import PartitionSpec as P

TOP = 32768.0
LEAST = 2.0**-40


def halves(count):
    inner = 2 if count % 2 == 0 else 1
    return count // inner, inner


def outer_moves(count):
    outer, inner = halves(count)

    def perm(to):
        return [(i, to(i // inner) * inner + i % inner) for i in range(count)]

    moves = []
    if outer & (outer - 1) == 0:
        held, stride = 1, outer // 2
        while stride:
            moves += [(b, perm(lambda o, s=stride: o ^ s)) for b in range(held)]
            held, stride = 2 * held, stride // 2
    else:
        moves = [(0, perm(lambda o, s=s: (o + s) % outer)) for s in range(1, outer)]
    return moves


def inner_shift(count, step):
    _, inner = halves(count)
    return [(i, i // inner * inner + (i + step) % inner) for i in range(count)]


def square_shift(n_row, n_col, j, k):
    r_outer, r_inner = halves(n_row)
    _, c_inner = halves(n_col)
    pairs = []
    for r in range(n_row):
        for c in range(n_col):
            to_r = (r // r_inner + j) % r_outer * r_inner + r % r_inner
            to_c = c // c_inner * c_inner + (c + k) % c_inner
            pairs.append((r * n_col + c, to_r * n_col + to_c))
    return pairs


def dot(a, b, dims):
    return lax.dot_general(a, b, (dims, ((), ())), preferred_element_type=jnp.float32)


def join(refs):
    return jnp.concatenate([ref[s] for s in range(2) for ref in refs], axis=0)


def weigh(rows, keys, factors):
    n, m = rows.shape[0] // 2, keys.shape[0] // 2
    scores = dot(rows, keys, ((1,), (1,)))
    cross = scores[:n, m:] - scores[n:, :m]
    inmodal = scores[:n, :m] - scores[n:, m:]
    p_mat = (cross * factors[0:1, 0:1]).astype(jnp.bfloat16)
    q_mat = (inmodal * factors[1:2, 0:1]).astype(jnp.bfloat16)
    return p_mat, q_mat


def tiles(width):
    step = 256 if width % 256 == 0 else width
    return [slice(i, i + step) for i in range(0, width, step)]


def spread(p_mat, q_mat):
    return jnp.concatenate(
        [jnp.concatenate([q_mat, p_mat], axis=1), jnp.concatenate([-p_mat, -q_mat], axis=1)], axis=0
    )


def bounds(rows, factors, total):
    size = jnp.sum(jnp.abs(rows.astype(jnp.float32)), axis=1, keepdims=True)
    size = size[: size.shape[0] // 2] + size[size.shape[0] // 2 :]
    return size * ((factors[0:1, 0:1] + factors[1:2, 0:1]) * (1.02 * total)) + 1e-25


def largest(keys):
    return jnp.max(jnp.max(jnp.abs(keys.astype(jnp.float32)), axis=0, keepdims=True), axis=1, keepdims=True)


def early_kernel(total, n, factors, *refs):
    own, acc, up, down, most_key = refs[-5:]
    rows = join(refs[:n])
    own[...] = rows
    keys = join(refs[n:-5])
    mix = spread(*weigh(rows, keys, factors))
    for at in tiles(keys.shape[1]):
        acc[:, at] = dot(mix, keys[:, at], ((1,), (0,)))
    most = bounds(rows, factors, total)
    half = most.shape[0]
    for s in range(2):
        up[s * half : (s + 1) * half] = jnp.broadcast_to(TOP / most, (half, up.shape[1]))
    down[...] = jnp.broadcast_to((most / TOP)[: down.shape[0]], down.shape)
    most_key[...] = jnp.broadcast_to(largest(keys), most_key.shape)


def late_kernel(total, n, m, factors, own, acc, up, most_key, *refs):
    last, outs = refs[0], refs[-n - 1 :]
    early, late = join(refs[1 : m + 1]), join(refs[m + 1 : -n - 1])
    rows, width = last.shape[1:]
    half = n * rows
    rest = join([last])
    every = jnp.concatenate([own[:half], last[0], own[half:], last[1]], axis=0)
    mix = spread(*weigh(every, late, factors))
    mix_rest = spread(*weigh(rest, early, factors))
    magnitude = jnp.maximum(jnp.maximum(largest(late), most_key[0:1, 0:1]), LEAST)
    exponent = jnp.ceil(jnp.log2(magnitude))
    shrink = jnp.exp2(-2.0 * exponent)
    factor = TOP / bounds(rest, factors, total)

    def send(out, s, at, values):
        across = width // 128
        for r in range(0, rows, 8):
            for c in range(0, values.shape[1], 128):
                tile = (s * rows + r) // 8 * across + (at.start + c) // 128
                out[tile] = values[r : r + 8, c : c + 128]

    for out in outs[1:]:
        out[out.shape[0] - 1] = jnp.broadcast_to(exponent, (8, 128))
    for at in tiles(width):
        grad = dot(mix, late[:, at], ((1,), (0,)))
        grad_rest = dot(mix_rest, early[:, at], ((1,), (0,)))
        for s in range(2):
            low = s * (half + rows)
            mine = slice(s * half, (s + 1) * half)
            ready = grad[low : low + half] + acc[mine, at]
            outs[0][s, :, at] = ready[:rows]
            ready = ready * up[mine, :1] * shrink
            for i in range(1, n):
                send(outs[i], s, at, ready[i * rows : (i + 1) * rows])
            both = grad[low + half : low + half + rows] + grad_rest[s * rows : (s + 1) * rows]
            send(outs[n], s, at, both * factor * shrink)


def sum_kernel(own, down, *refs):
    *parts, images, texts = refs
    rows, width = images.shape
    across = width // 128
    grow = [jnp.exp2(2.0 * part[part.shape[0] - 1]) for part in parts]
    for s, out in enumerate((images, texts)):
        for r in range(0, rows, 8):
            scales = [down[r : r + 8] * g for g in grow]
            for c in range(across):
                total = own[s, r : r + 8, c * 128 : (c + 1) * 128]
                for part, scale in zip(parts, scales):
                    total = total + part[(s * rows + r) // 8 * across + c] * scale
                out[r : r + 8, c * 128 : (c + 1) * 128] = total


def call(kernel, operands, out_shape, flops):
    vmem = pl.BlockSpec(memory_space=pltpu.VMEM)
    moved = sum(x.size * x.dtype.itemsize for x in [*operands, *out_shape])
    return pl.pallas_call(
        kernel,
        out_shape=out_shape,
        in_specs=[vmem] * len(operands),
        out_specs=[vmem] * len(out_shape),
        compiler_params=pltpu.CompilerParams(vmem_limit_bytes=40 * 2**20),
        cost_estimate=pl.CostEstimate(flops=flops, bytes_accessed=moved, transcendentals=0),
    )(*operands)


def local(images, texts, loss_weights):
    n_row, n_col = lax.axis_size("row"), lax.axis_size("col")
    row_inner = halves(n_row)[1]
    rows, width = images.shape
    batch = rows * n_row * n_col
    factors = jnp.broadcast_to((loss_weights * (1.0 / math.sqrt(width * batch)))[:, None], (2, 128))
    both = ("row", "col")
    square = [(j, k) for j in range(halves(n_row)[0]) for k in range(halves(n_col)[1])]
    square = sorted(square[1:], key=lambda place: (all(place), not place[0]))
    own = jnp.stack([images, texts])

    mine = [own] + [lax.ppermute(own, both, square_shift(n_row, n_col, j, k)) for j, k in square]

    line, apart = [own], {0: [images, texts]}
    for step, (which, perm) in enumerate(outer_moves(n_col), 1):
        if which in apart and (which or step == 1):
            apart[step] = [lax.ppermute(half, "col", perm) for half in apart[which]]
            line.append(jnp.stack(apart[step]))
        else:
            line.append(lax.ppermute(line[which], "col", perm))

    def pair(block):
        return [lax.ppermute(block, "row", inner_shift(n_row, k)) for k in range(1, row_inner)]

    early, copies = line[:-1], []
    for i, block in enumerate(line[:-1]):
        if i == 0 and len(mine) > 1:
            block, mine[1] = lax.optimization_barrier((block, mine[1]))
        if i == 1 and len(early) > 2:
            block, mine[1], early[2] = lax.optimization_barrier((block, mine[1], early[2]))
        copies += pair(block)
    total = rows * len(line) * row_inner
    f32 = jnp.float32
    *first, last = mine
    many = rows * len(first)

    def flops(blocks, keys):
        return 16 * rows * width * rows * blocks * keys

    mine_joined, acc, up, down, most_key = call(
        functools.partial(early_kernel, total, len(first)),
        [factors] + first + early,
        [jax.ShapeDtypeStruct((2 * many, width), images.dtype)]
        + [jax.ShapeDtypeStruct(s, f32) for s in [(2 * many, width), (2 * many, 128), (rows, 128), (8, 128)]],
        flops(len(first), len(early)),
    )
    late = copies + [line[-1]] + pair(line[-1])
    parts = call(
        functools.partial(late_kernel, total, len(first), len(early)),
        [factors, mine_joined, acc, up, most_key, last] + early + late,
        [jax.ShapeDtypeStruct((2, rows, width), f32)]
        + [jax.ShapeDtypeStruct((2 * rows * width // 1024 + 1, 8, 128), f32)] * len(square),
        flops(len(first), len(late)) + flops(1, len(early + late)),
    )
    far = sorted(zip(square, parts[1:]), key=lambda item: sum(item[0]))
    back = [
        lax.ppermute(part.astype(jnp.float16), both, square_shift(n_row, n_col, -j, -k)) for (j, k), part in far
    ]
    return tuple(
        call(
            sum_kernel,
            [parts[0], down] + [part.astype(f32) for part in back],
            [jax.ShapeDtypeStruct((rows, width), f32)] * 2,
            4 * rows * width * len(mine),
        )
    )


def solution(mesh):
    in_specs = (P(("row", "col"), None), P(("row", "col"), None), P())
    out_specs = (P(("row", "col"), None), P(("row", "col"), None))
    return jax.shard_map(local, mesh=mesh, in_specs=in_specs, out_specs=out_specs, check_vma=False)
```

```python
import functools
import math

import jax
import jax.numpy as jnp
from jax import lax
from jax.experimental import pallas as pl
from jax.experimental.pallas import tpu as pltpu
from jax.sharding import PartitionSpec as P

TOP = 32768.0
LEAST = 2.0**-40


def halves(count):
    inner = 2 if count % 2 == 0 else 1
    return count // inner, inner


def outer_moves(count):
    outer, inner = halves(count)

    def perm(to):
        return [(i, to(i // inner) * inner + i % inner) for i in range(count)]

    moves = []
    if outer & (outer - 1) == 0:
        held, stride = 1, outer // 2
        while stride:
            moves += [(b, perm(lambda o, s=stride: o ^ s)) for b in range(held)]
            held, stride = 2 * held, stride // 2
    else:
        moves = [(0, perm(lambda o, s=s: (o + s) % outer)) for s in range(1, outer)]
    return moves


def inner_shift(count, step):
    _, inner = halves(count)
    return [(i, i // inner * inner + (i + step) % inner) for i in range(count)]


def square_shift(n_row, n_col, j, k):
    r_outer, r_inner = halves(n_row)
    _, c_inner = halves(n_col)
    pairs = []
    for r in range(n_row):
        for c in range(n_col):
            to_r = (r // r_inner + j) % r_outer * r_inner + r % r_inner
            to_c = c // c_inner * c_inner + (c + k) % c_inner
            pairs.append((r * n_col + c, to_r * n_col + to_c))
    return pairs


def dot(a, b, dims):
    return lax.dot_general(a, b, (dims, ((), ())), preferred_element_type=jnp.float32)


def join(refs):
    return jnp.concatenate([ref[s] for s in range(2) for ref in refs], axis=0)


def weigh(rows, keys, factors):
    n, m = rows.shape[0] // 2, keys.shape[0] // 2
    scores = dot(rows, keys, ((1,), (1,)))
    cross = scores[:n, m:] - scores[n:, :m]
    inmodal = scores[:n, :m] - scores[n:, m:]
    p_mat = (cross * factors[0:1, 0:1]).astype(jnp.bfloat16)
    q_mat = (inmodal * factors[1:2, 0:1]).astype(jnp.bfloat16)
    return p_mat, q_mat


def tiles(width):
    step = 256 if width % 256 == 0 else width
    return [slice(i, i + step) for i in range(0, width, step)]


def spread(p_mat, q_mat):
    return jnp.concatenate(
        [jnp.concatenate([q_mat, p_mat], axis=1), jnp.concatenate([-p_mat, -q_mat], axis=1)], axis=0
    )


def bounds(rows, factors, total):
    size = jnp.sum(jnp.abs(rows.astype(jnp.float32)), axis=1, keepdims=True)
    size = size[: size.shape[0] // 2] + size[size.shape[0] // 2 :]
    return size * ((factors[0:1, 0:1] + factors[1:2, 0:1]) * (1.02 * total)) + 1e-25


def largest(keys):
    return jnp.max(jnp.max(jnp.abs(keys.astype(jnp.float32)), axis=0, keepdims=True), axis=1, keepdims=True)


def early_kernel(total, n, factors, *refs):
    own, acc, up, down, most_key = refs[-5:]
    rows = join(refs[:n])
    own[...] = rows
    keys = join(refs[n:-5])
    mix = spread(*weigh(rows, keys, factors))
    for at in tiles(keys.shape[1]):
        acc[:, at] = dot(mix, keys[:, at], ((1,), (0,)))
    most = bounds(rows, factors, total)
    half = most.shape[0]
    for s in range(2):
        up[s * half : (s + 1) * half] = jnp.broadcast_to(TOP / most, (half, up.shape[1]))
    down[...] = jnp.broadcast_to((most / TOP)[: down.shape[0]], down.shape)
    most_key[...] = jnp.broadcast_to(largest(keys), most_key.shape)


def late_kernel(total, n, m, factors, own, acc, up, most_key, *refs):
    last, outs = refs[0], refs[-n - 1 :]
    early, late = join(refs[1 : m + 1]), join(refs[m + 1 : -n - 1])
    rows, width = last.shape[1:]
    half = n * rows
    rest = join([last])
    every = jnp.concatenate([own[:half], last[0], own[half:], last[1]], axis=0)
    mix = spread(*weigh(every, late, factors))
    mix_rest = spread(*weigh(rest, early, factors))
    magnitude = jnp.maximum(jnp.maximum(largest(late), most_key[0:1, 0:1]), LEAST)
    exponent = jnp.ceil(jnp.log2(magnitude))
    shrink = jnp.exp2(-2.0 * exponent)
    factor = TOP / bounds(rest, factors, total)

    def send(out, s, at, values):
        across = width // 128
        for r in range(0, rows, 8):
            for c in range(0, values.shape[1], 128):
                tile = (s * rows + r) // 8 * across + (at.start + c) // 128
                out[tile] = values[r : r + 8, c : c + 128]

    for out in outs[1:]:
        out[out.shape[0] - 1] = jnp.broadcast_to(exponent, (8, 128))
    for at in tiles(width):
        grad = dot(mix, late[:, at], ((1,), (0,)))
        grad_rest = dot(mix_rest, early[:, at], ((1,), (0,)))
        for s in range(2):
            low = s * (half + rows)
            mine = slice(s * half, (s + 1) * half)
            ready = grad[low : low + half] + acc[mine, at]
            outs[0][s, :, at] = ready[:rows]
            ready = ready * up[mine, :1] * shrink
            for i in range(1, n):
                send(outs[i], s, at, ready[i * rows : (i + 1) * rows])
            both = grad[low + half : low + half + rows] + grad_rest[s * rows : (s + 1) * rows]
            send(outs[n], s, at, both * factor * shrink)


def sum_kernel(own, down, *refs):
    *parts, images, texts = refs
    rows, width = images.shape
    across = width // 128
    grow = [jnp.exp2(2.0 * part[part.shape[0] - 1]) for part in parts]
    for s, out in enumerate((images, texts)):
        for r in range(0, rows, 8):
            scales = [down[r : r + 8] * g for g in grow]
            for c in range(across):
                total = own[s, r : r + 8, c * 128 : (c + 1) * 128]
                for part, scale in zip(parts, scales):
                    total = total + part[(s * rows + r) // 8 * across + c] * scale
                out[r : r + 8, c * 128 : (c + 1) * 128] = total


def call(kernel, operands, out_shape, flops):
    vmem = pl.BlockSpec(memory_space=pltpu.VMEM)
    moved = sum(x.size * x.dtype.itemsize for x in [*operands, *out_shape])
    return pl.pallas_call(
        kernel,
        out_shape=out_shape,
        in_specs=[vmem] * len(operands),
        out_specs=[vmem] * len(out_shape),
        compiler_params=pltpu.CompilerParams(vmem_limit_bytes=40 * 2**20),
        cost_estimate=pl.CostEstimate(flops=flops, bytes_accessed=moved, transcendentals=0),
    )(*operands)


def local(images, texts, loss_weights):
    n_row, n_col = lax.axis_size("row"), lax.axis_size("col")
    row_inner = halves(n_row)[1]
    rows, width = images.shape
    batch = rows * n_row * n_col
    factors = jnp.broadcast_to((loss_weights * (1.0 / math.sqrt(width * batch)))[:, None], (2, 128))
    both = ("row", "col")
    square = [(j, k) for j in range(halves(n_row)[0]) for k in range(halves(n_col)[1])]
    square = sorted(square[1:], key=lambda place: (all(place), not place[0]))
    own = jnp.stack([images, texts])

    mine = [own] + [lax.ppermute(own, both, square_shift(n_row, n_col, j, k)) for j, k in square]

    line, apart = [own], {0: [images, texts]}
    for step, (which, perm) in enumerate(outer_moves(n_col), 1):
        if which in apart and (which or step == 1):
            apart[step] = [lax.ppermute(half, "col", perm) for half in apart[which]]
            line.append(jnp.stack(apart[step]))
        else:
            line.append(lax.ppermute(line[which], "col", perm))

    def pair(block):
        return [lax.ppermute(block, "row", inner_shift(n_row, k)) for k in range(1, row_inner)]

    early, copies = line[:-1], []
    for i, block in enumerate(line[:-1]):
        if i == 0 and len(mine) > 1:
            block, mine[1] = lax.optimization_barrier((block, mine[1]))
        if i == 1 and len(early) > 2:
            block, mine[1], early[2] = lax.optimization_barrier((block, mine[1], early[2]))
        copies += pair(block)
    total = rows * len(line) * row_inner
    f32 = jnp.float32
    *first, last = mine
    many = rows * len(first)

    def flops(blocks, keys):
        return 16 * rows * width * rows * blocks * keys

    mine_joined, acc, up, down, most_key = call(
        functools.partial(early_kernel, total, len(first)),
        [factors] + first + early,
        [jax.ShapeDtypeStruct((2 * many, width), images.dtype)]
        + [jax.ShapeDtypeStruct(s, f32) for s in [(2 * many, width), (2 * many, 128), (rows, 128), (8, 128)]],
        flops(len(first), len(early)),
    )
    late = copies + [line[-1]] + [jnp.stack(halves) for halves in zip(*map(pair, apart.get(len(line) - 1, line[-1])))]
    parts = call(
        functools.partial(late_kernel, total, len(first), len(early)),
        [factors, mine_joined, acc, up, most_key, last] + early + late,
        [jax.ShapeDtypeStruct((2, rows, width), f32)]
        + [jax.ShapeDtypeStruct((2 * rows * width // 1024 + 1, 8, 128), f32)] * len(square),
        flops(len(first), len(late)) + flops(1, len(early + late)),
    )
    far = sorted(zip(square, parts[1:]), key=lambda item: sum(item[0]))
    back = [
        lax.ppermute(part.astype(jnp.float16), both, square_shift(n_row, n_col, -j, -k)) for (j, k), part in far
    ]
    return tuple(
        call(
            sum_kernel,
            [parts[0], down] + [part.astype(f32) for part in back],
            [jax.ShapeDtypeStruct((rows, width), f32)] * 2,
            4 * rows * width * len(mine),
        )
    )


def solution(mesh):
    in_specs = (P(("row", "col"), None), P(("row", "col"), None), P())
    out_specs = (P(("row", "col"), None), P(("row", "col"), None))
    return jax.shard_map(local, mesh=mesh, in_specs=in_specs, out_specs=out_specs, check_vma=False)
```
